256 devices in a mesh: dp: 16 (over z_hi, x), seq: 16 (over y, z_lo, core).
Axes of the slice: x: 4, y: 4, z: 8 (z_hi: 4, z_lo: 2; z = z_hi * 2 + z_lo), core: 2. Of those that a mesh axis runs over, the one named last changes fastest.
Arguments:
- queries: bfloat16 [16, 4096, 1024], P('dp', 'seq'), may hold values from -4.5 to 4.5
- keys: bfloat16 [16, 4096, 1024], P('dp', 'seq'), may hold values from -4.5 to 4.5
- values: bfloat16 [16, 4096, 1024], P('dp', 'seq'), may hold values from -6 to 6
- d_out: bfloat16 [16, 4096, 2048], P('dp', 'seq'), may hold values from -6 to 6
- w_out: bfloat16 [2048, 1024], replicated, may hold values from -0.1875 to 0.1875
Outputs:
- d_queries: bfloat16 [16, 4096, 1024], P('dp', 'seq')
- d_keys: bfloat16 [16, 4096, 1024], P('dp', 'seq')
- d_values: bfloat16 [16, 4096, 1024], P('dp', 'seq')
- d_weight: float32 [2048, 1024], P('seq')
The draws below stay inside these ranges and needn't reach their ends.
All inputs are finite; a program needn't handle non-finite values.
Results may differ from the reference program's by a relative error of at most 0.024.
Values may be sent and summed in bfloat16 or wider, within the bound.
No kernel may reach another device: no remote copies, remote signals or barrier semaphores. Data moves between devices by JAX's collectives and lax.ppermute only.
A program may use at most 128 MiB of HBM per device.

```python
import jax
import jax.numpy as jnp
from jax import lax

D = 2048
HEADS = 8
HDIM = 128
BLOCK = 128
HD = 1024
TOKENS = 4096
SEQS = 16
LEVELS = 5


def draw_queries(key, part):
    key = jax.random.fold_in(key, 1)
    return jnp.clip(jax.random.normal(key, (SEQS, TOKENS, HD), jnp.float32), -4.5, 4.5).astype(jnp.bfloat16)


def draw_keys(key, part):
    key = jax.random.fold_in(key, 2)
    return jnp.clip(jax.random.normal(key, (SEQS, TOKENS, HD), jnp.float32), -4.5, 4.5).astype(jnp.bfloat16)


def spiked(result, stream_key, source, target, blocks, factor):
    def block_of(dim):
        return (jnp.arange(result.shape[dim]) // (result.shape[dim] // blocks)).reshape((-1,) + (1,) * (result.ndim - 1 - dim))

    first = jax.random.permutation(stream_key, blocks)[block_of(target)]
    far = (block_of(target) + blocks // 2) % blocks
    return jnp.where((block_of(source) == first) | (block_of(source) == far), factor * result, result)


def block_scale(own_key, shape, pieces, smallest, high):
    gain = 1.0
    for position, parts in pieces:
        draws = jax.random.uniform(jax.random.fold_in(jax.random.fold_in(own_key, 6), position), (parts,), jnp.float32, smallest / len(pieces), high / len(pieces))
        gain = gain * jnp.repeat(jnp.exp(draws), shape[position] // parts).reshape((-1,) + (1,) * (len(shape) - 1 - position))
    return gain


def scatter_about(rng, shape, spread, most, pieces=(), kind=jnp.bfloat16):
    array = spread * jax.random.normal(rng, shape, jnp.float32)
    if pieces:
        array = array * block_scale(rng, shape, pieces, -0.22, 0.18)
    return jnp.clip(array, -most, most).astype(kind)


def heavy_noise(key, shape, scale, limit, pieces, heavy, kind=jnp.bfloat16):
    drawn = scale * jax.random.normal(key, shape, jnp.float32)
    if pieces:
        drawn = drawn * block_scale(key, shape, pieces, -0.22, 0.18)
    return jnp.clip(spiked(drawn, jax.random.fold_in(key, 3), *heavy), -limit, limit).astype(kind)


def setup_inputs(seed: int = 0) -> dict:
    arg_keys = jax.random.split(jax.random.key(seed), 6)
    queries = draw_queries(jax.random.fold_in(arg_keys[5], 71), 0)
    keys = draw_keys(jax.random.fold_in(arg_keys[5], 71), 0)
    values = scatter_about(arg_keys[2], (SEQS, TOKENS, HD), 1.0, 6.0, ((0, 16), (1, 16)))
    d_out = heavy_noise(arg_keys[3], (SEQS, TOKENS, D), 1.0, 6.0, ((0, 16), (1, 16)), (1, 2, 16, 2.0))
    w_out = scatter_about(arg_keys[4], (D, HD), HD ** -0.5, 0.1875)
    return dict(queries=queries, keys=keys, values=values, d_out=d_out, w_out=w_out)


def to_half(tensor):
    return lax.optimization_barrier(tensor.astype(jnp.bfloat16))


def coarsen(matrix):
    paired_rows = matrix.astype(jnp.float32).reshape(matrix.shape[0] // 2, 2, matrix.shape[1])
    return to_half((paired_rows[:, 0] + paired_rows[:, 1]) * 0.5)


def flip_pairs(tensor):
    layout = tensor.shape
    return tensor.reshape((layout[0] // 2, 2) + layout[1:])[:, ::-1].reshape(layout)


def to_tokens(tensor):
    return jnp.transpose(tensor, (1, 0, 2)).reshape(tensor.shape[1], -1)


def to_groups(tensor, groups):
    return jnp.transpose(tensor.reshape(tensor.shape[0], groups, -1), (1, 0, 2))


def one_sequence(queries, keys, values, d_out, w_out):
    score_scale = HDIM ** -0.5
    coarse_q = [queries]
    coarse_k = [keys]
    coarse_v = [values]
    for height in range(1, LEVELS):
        coarse_q.append(coarsen(coarse_q[-1]))
        coarse_k.append(coarsen(coarse_k[-1]))
        coarse_v.append(coarsen(coarse_v[-1]))
    level_data = []
    for height in range(LEVELS):
        groups = coarse_q[height].shape[0] // BLOCK
        q_heads = coarse_q[height].astype(jnp.float32).reshape(groups, BLOCK, HEADS, HDIM)
        k_heads = coarse_k[height].astype(jnp.float32).reshape(groups, BLOCK, HEADS, HDIM)
        v_heads = coarse_v[height].astype(jnp.float32).reshape(groups, BLOCK, HEADS, HDIM)
        if height == 0:
            k_group = jnp.concatenate([k_heads, flip_pairs(k_heads)], axis=1)
            v_group = jnp.concatenate([v_heads, flip_pairs(v_heads)], axis=1)
        else:
            k_group = flip_pairs(k_heads)
            v_group = flip_pairs(v_heads)
        level_data.append((q_heads, k_group, v_group))
    raw_list = []
    row_peak = None
    for height, (q_heads, k_group, v_group) in enumerate(level_data):
        raw_scores = jnp.einsum('grhd,gjhd->ghrj', q_heads, k_group) * score_scale
        level_peak = to_tokens(jnp.repeat(jnp.max(raw_scores, axis=3), 2 ** height, axis=2))
        row_peak = level_peak if height == 0 else jnp.maximum(row_peak, level_peak)
        raw_list.append(raw_scores)
    normaliser = jnp.zeros((HEADS, TOKENS), jnp.float32)
    numerator = jnp.zeros((TOKENS, HEADS, HDIM), jnp.float32)
    weight_list = []
    for height, (q_heads, k_group, v_group) in enumerate(level_data):
        groups = q_heads.shape[0]
        weights = (2.0 ** height) * jnp.exp(jnp.repeat(raw_list[height], 2 ** height, axis=2) - to_groups(row_peak, groups)[..., None])
        normaliser = normaliser + to_tokens(jnp.sum(weights, axis=3))
        numerator = numerator + jnp.einsum('ghfj,gjhd->gfhd', to_half(weights).astype(jnp.float32), v_group).reshape(TOKENS, HEADS, HDIM)
        weight_list.append(weights)
    attended = to_half(numerator / jnp.transpose(normaliser)[:, :, None]).reshape(TOKENS, HD)
    d_attended = to_half(jnp.dot(d_out, w_out, preferred_element_type=jnp.float32))
    weight_term = jnp.dot(jnp.transpose(d_out), attended, preferred_element_type=jnp.float32)
    dout_heads = d_attended.astype(jnp.float32).reshape(TOKENS, HEADS, HDIM)
    row_delta = jnp.transpose(jnp.sum(dout_heads * attended.astype(jnp.float32).reshape(TOKENS, HEADS, HDIM), axis=2))
    grad_q = []
    grad_k = []
    grad_v = []
    for height, (q_heads, k_group, v_group) in enumerate(level_data):
        groups = q_heads.shape[0]
        q_rows = q_heads.shape[1]
        repeats = 2 ** height
        key_count = k_group.shape[1]
        probability = weight_list[height] / to_groups(normaliser, groups)[..., None]
        dout_group = dout_heads.reshape(groups, -1, HEADS, HDIM)
        prob_grad = jnp.einsum('gfhd,gjhd->ghfj', dout_group, v_group)
        score_grad = probability * (prob_grad - to_groups(row_delta, groups)[..., None])
        value_part = jnp.einsum('ghfj,gfhd->gjhd', to_half(probability).astype(jnp.float32), dout_group)
        coarse_grad = to_half(jnp.sum(score_grad.reshape(groups, HEADS, q_rows, repeats, key_count), axis=3)).astype(jnp.float32)
        grad_q.append((jnp.einsum('ghrj,gjhd->grhd', coarse_grad, k_group) * score_scale).reshape(-1, HD))
        key_part = jnp.einsum('ghrj,grhd->gjhd', coarse_grad, q_heads) * score_scale
        if height == 0:
            grad_k.append((key_part[:, :BLOCK] + flip_pairs(key_part[:, BLOCK:])).reshape(-1, HD))
            grad_v.append((value_part[:, :BLOCK] + flip_pairs(value_part[:, BLOCK:])).reshape(-1, HD))
        else:
            grad_k.append(flip_pairs(key_part).reshape(-1, HD))
            grad_v.append(flip_pairs(value_part).reshape(-1, HD))
    for height in range(LEVELS - 1, 0, -1):
        grad_q[height - 1] = grad_q[height - 1] + jnp.repeat(grad_q[height] * 0.5, 2, axis=0)
        grad_k[height - 1] = grad_k[height - 1] + jnp.repeat(grad_k[height] * 0.5, 2, axis=0)
        grad_v[height - 1] = grad_v[height - 1] + jnp.repeat(grad_v[height] * 0.5, 2, axis=0)
    return grad_q[0].astype(jnp.bfloat16), grad_k[0].astype(jnp.bfloat16), grad_v[0].astype(jnp.bfloat16), weight_term


def reference(queries, keys, values, d_out, w_out):
    def per_sequence(running, sequence):
        grad_query, grad_key, grad_value, weight_term = one_sequence(sequence[0], sequence[1], sequence[2], sequence[3], w_out)
        return running + weight_term, (grad_query, grad_key, grad_value)

    d_weight, outputs = lax.scan(per_sequence, jnp.zeros((D, HD), jnp.float32), (queries, keys, values, d_out))
    return outputs[0], outputs[1], outputs[2], d_weight
```

```python
import functools

import jax
import jax.numpy as jnp
from jax import lax
from jax.experimental import pallas as pl
from jax.experimental.pallas import tpu as pltpu
from jax.sharding import PartitionSpec as P

HEADS = 8
HDIM = 128
ROWS = 256
WIDTH = 1024
DMODEL = 2048
SCALE = HDIM**-0.5
LEVEL_ROWS = (128, 64, 32, 16)
LEVEL_AT = (0, 128, 192, 224)
COARSE = 240
BF = jnp.bfloat16
F32 = jnp.float32
VMEM = pltpu.CompilerParams(vmem_limit_bytes=48 * 1024 * 1024)

CORE, ZLO, Y1, Y2, Y3 = 1, 2, 4, 8, 12
X1, X2, X3, ZH1, ZH3 = 1, 2, 3, 4, 12


def swap(value, axis, mask):
    pairs = [(source, source ^ mask) for source in range(16)]
    return lax.ppermute(value, axis, pairs)


def dot(a, b):
    return jnp.dot(a, b, preferred_element_type=F32)


def dot_nt(a, b):
    return lax.dot_general(a, b, (((1,), (1,)), ((), ())), preferred_element_type=F32)


def dot_tn(a, b):
    return lax.dot_general(a, b, (((0,), (0,)), ((), ())), preferred_element_type=F32)


def pool_matrix(rows):
    r = lax.broadcasted_iota(jnp.int32, (rows, 2 * rows), 0)
    c = lax.broadcasted_iota(jnp.int32, (rows, 2 * rows), 1)
    return jnp.where((c == 2 * r) | (c == 2 * r + 1), 0.5, 0.0).astype(BF)


def coarse_levels(x):
    levels = []
    for rows in LEVEL_ROWS:
        x = dot(pool_matrix(rows), x).astype(BF)
        levels.append(x)
    return levels


def rep2(buf, x):
    rows, cols = x.shape
    buf[pl.ds(0, rows, stride=2), 0:cols] = x
    buf[pl.ds(1, rows, stride=2), 0:cols] = x
    return buf[0 : 2 * rows, 0:cols]


def pairsum(buf, x):
    rows, cols = x.shape
    buf[0:rows, 0:cols] = x
    half = rows // 2
    return buf[pl.ds(0, half, stride=2), 0:cols] + buf[pl.ds(1, half, stride=2), 0:cols]


def wide(column):
    return jnp.broadcast_to(column, (column.shape[0], HDIM))


def coarsen_kernel(k_ref, v_ref, o1, o2, o3, o4):
    ks = coarse_levels(k_ref[...])
    vs = coarse_levels(v_ref[...])
    for out, rows, k, v in zip((o1, o2, o3, o4), LEVEL_ROWS, ks, vs):
        out[0:rows, :] = k
        out[rows : 2 * rows, :] = v


def arrange_kernel(at_ref, dout_ref, own_ref, other_ref):
    y, zl, c = at_ref[0], at_ref[1], at_ref[2]
    for n in range(8):
        jy, iz = n // 2, n % 2
        base = (y ^ jy) * 4 + (zl ^ iz) * 2
        for ref, core in ((own_ref, c), (other_ref, 1 - c)):
            at = pl.multiple_of((base + core) * 128, 128)
            block = dout_ref[:, pl.ds(at, 128)]
            ref[n * 128 : (n + 1) * 128, :] = block.T


def local_kernel(q_ref, k_ref, v_ref, dout_ref, w_ref, datt_ref, qc_ref, n_ref, m_ref, l_ref):
    datt_ref[...] = dot(dout_ref[...], w_ref[...]).astype(BF)
    q = q_ref[...]
    for x, at, rows in zip(coarse_levels(q), LEVEL_AT, LEVEL_ROWS):
        qc_ref[at : at + rows, :] = x
    for h in range(q.shape[1] // HDIM):
        cols = slice(h * HDIM, (h + 1) * HDIM)
        s = dot_nt(q_ref[:, cols], k_ref[:, cols]) * SCALE
        m = jnp.max(s, axis=1, keepdims=True)
        e = jnp.exp(s - m)
        l_ref[:, cols] = wide(jnp.sum(e, axis=1, keepdims=True))
        m_ref[:, cols] = wide(m)
        n_ref[:, cols] = dot(e.astype(BF), v_ref[:, cols])


def sibling(level, a_ref, u_ref, e_ref, cols):
    if level == 1:
        return a_ref[0:128, cols], a_ref[128:256, cols]
    spans = {
        2: ((0, 64),),
        3: ((128, 32), (256, 32)),
        4: ((192, 16), (224, 16), (320, 16), (352, 16)),
    }[level]
    keys = [ref[at : at + n, cols] for ref in (u_ref, e_ref) for at, n in spans]
    vals = [ref[at + n : at + 2 * n, cols] for ref in (u_ref, e_ref) for at, n in spans]
    return jnp.concatenate(keys, axis=0), jnp.concatenate(vals, axis=0)


def forward_kernel(
    qc_ref, a_ref, u_ref, e_ref, n_ref, m_ref, l_ref,
    att_ref, lse_ref, w_ref, f_ref, c_ref, bufs,
):
    for h in range(qc_ref.shape[1] // HDIM):
        cols = slice(h * HDIM, (h + 1) * HDIM)
        per = []
        for level in range(1, 5):
            at, rows = LEVEL_AT[level - 1], LEVEL_ROWS[level - 1]
            keys, vals = sibling(level, a_ref, u_ref, e_ref, cols)
            s = dot_nt(qc_ref[at : at + rows, cols], keys) * SCALE
            m = jnp.max(s, axis=1, keepdims=True)
            e = jnp.exp(s - m)
            w_ref[at : at + rows, cols] = e
            per.append((wide(m), wide(jnp.sum(e, axis=1, keepdims=True)), dot(e.astype(BF), vals)))
        top, total, num = per[3]
        total, num = total * 16.0, num * 16.0
        for level in (3, 2, 1):
            at, rows = LEVEL_AT[level - 1], LEVEL_ROWS[level - 1]
            m, lsum, n = per[level - 1]
            up_m = rep2(bufs.at[3 * h], top)
            up_l = rep2(bufs.at[3 * h + 1], total)
            up_n = rep2(bufs.at[3 * h + 2], num)
            top = jnp.maximum(m, up_m)
            own = jnp.exp(m - top) * 2.0**level
            far = jnp.exp(up_m - top)
            total = own * lsum + far * up_l
            num = own * n + far * up_n
            c_ref[at : at + rows, cols] = own
            f_ref[256 + at : 256 + at + rows, cols] = far
        up_m = rep2(bufs.at[3 * h], top)
        up_l = rep2(bufs.at[3 * h + 1], total)
        up_n = rep2(bufs.at[3 * h + 2], num)
        m = m_ref[:, cols]
        top = jnp.maximum(m, up_m)
        own = jnp.exp(m - top)
        far = jnp.exp(up_m - top)
        total = own * l_ref[:, cols] + far * up_l
        inv = 1.0 / total
        att_ref[:, cols] = ((own * n_ref[:, cols] + far * up_n) * inv).astype(BF)
        f_ref[0:256, cols] = far * inv
        lse_ref[:, cols] = top + jnp.log(total)


def coarse_back_kernel(
    qc_ref, a_ref, u_ref, e_ref, datt_ref, att_ref, w_ref, f_ref, c_ref,
    send_ref, keep_ref, gq_ref, bufs,
):
    spans = {
        2: ((0, 64),),
        3: ((128, 32), (256, 32)),
        4: ((192, 16), (224, 16), (320, 16), (352, 16)),
    }
    for h in range(qc_ref.shape[1] // HDIM):
        cols = slice(h * HDIM, (h + 1) * HDIM)
        datt = datt_ref[:, cols].astype(F32)
        delta = wide(jnp.sum(datt * att_ref[:, cols].astype(F32), axis=1, keepdims=True))
        far = f_ref[0:256, cols]
        d, dl = far * datt, far * delta
        gqs = []
        for level in range(1, 5):
            at, rows = LEVEL_AT[level - 1], LEVEL_ROWS[level - 1]
            d = pairsum(bufs.at[2 * h], d)
            dl = pairsum(bufs.at[2 * h + 1], dl)
            keys, vals = sibling(level, a_ref, u_ref, e_ref, cols)
            if level < 4:
                own = c_ref[at : at + rows, cols]
                da, dd = (own * d).astype(BF), own * dl
                far = f_ref[256 + at : 256 + at + rows, cols]
                d, dl = far * d, far * dl
            else:
                da, dd = (16.0 * d).astype(BF), 16.0 * dl
            w = w_ref[at : at + rows, cols]
            ds = (w * (dot_nt(da, vals) - dd)).astype(BF)
            gqs.append(dot(ds, keys) * SCALE)
            gk = dot_tn(ds, qc_ref[at : at + rows, cols]) * SCALE
            gv = dot_tn(w.astype(BF), da)
            if level == 1:
                send_ref[0:128, cols] = gk.astype(BF)
                send_ref[128:256, cols] = gv.astype(BF)
            else:
                row = 0
                for ref, off in ((keep_ref, 0), (send_ref, 256)):
                    for start, n in spans[level]:
                        to = off + start
                        ref[to : to + n, cols] = gk[row : row + n].astype(ref.dtype)
                        ref[to + n : to + 2 * n, cols] = gv[row : row + n].astype(ref.dtype)
                        row += n
        g = gqs[3]
        for level in (3, 2, 1):
            g = gqs[level - 1] + rep2(bufs.at[2 * h], 0.5 * g)
        gq_ref[:, cols] = rep2(bufs.at[2 * h], 0.5 * g)


def weight_kernel(at_ref, own_ref, other_ref, att_ref, attp_ref, *outs):
    x = at_ref[3]

    def heads(ref, half):
        blocks = []
        for jx in range(4):
            col = pl.multiple_of(((x ^ jx) * 2 + half) * 128, 128)
            blocks.append(ref[:, pl.ds(col, 128)])
        return jnp.concatenate(blocks, axis=1)

    mine, theirs = heads(att_ref, 0), heads(attp_ref, 0)
    for j in range(4):
        rows = slice(j * 256, (j + 1) * 256)
        outs[j][...] = (dot(own_ref[rows, :], mine) + dot(other_ref[rows, :], theirs)).astype(BF)
    mine, theirs = heads(att_ref, 1), heads(attp_ref, 1)
    for j in range(4):
        rows = slice(j * 256, (j + 1) * 256)
        part = (dot(own_ref[rows, :], mine) + dot(other_ref[rows, :], theirs)).astype(BF)
        for jx in range(4):
            outs[4 + jx][rows, :] = part[:, jx * 128 : (jx + 1) * 128]


def sum_first_kernel(*refs):
    ins, outs = refs[:8], refs[8:]
    for j in range(4):
        cols = slice(j * 128, (j + 1) * 128)
        outs[j][...] = sum(r[:, cols].astype(F32) for r in ins[:4]).astype(BF)
    for j in range(4):
        rows = slice(j * 256, (j + 1) * 256)
        outs[4 + j][...] = sum(r[rows, :].astype(F32) for r in ins[4:]).astype(BF)


def sum_second_kernel(*refs):
    ins, (keep_ref, send_ref) = refs[:8], refs[8:]
    for half in range(2):
        cols = slice(half * 128, (half + 1) * 128)
        total = sum(r[...].astype(F32) for r in ins[4 * half : 4 * half + 4])
        keep_ref[:, cols] = total[0:128].astype(BF)
        send_ref[:, cols] = total[128:256].astype(BF)


def place_kernel(at_ref, a, b, c, d, out_ref):
    x = at_ref[3]
    for j, ref in enumerate((a, b, c, d)):
        col = pl.multiple_of((x ^ j) * 256, 256)
        out_ref[:, pl.ds(col, 256)] = ref[...].astype(F32)


def local_back_kernel(
    q_ref, k_ref, v_ref, datt_ref, att_ref, lse_ref, gqc_ref, dq_ref, gk_ref, gv_ref
):
    for h in range(q_ref.shape[1] // HDIM):
        cols = slice(h * HDIM, (h + 1) * HDIM)
        q, k, v, datt = q_ref[:, cols], k_ref[:, cols], v_ref[:, cols], datt_ref[:, cols]
        delta = jnp.sum(datt.astype(F32) * att_ref[:, cols].astype(F32), axis=1, keepdims=True)
        p = jnp.exp(dot_nt(q, k) * SCALE - lse_ref[:, cols][:, 0:1])
        ds = (p * (dot_nt(datt, v) - delta)).astype(BF)
        dq_ref[:, cols] = (dot(ds, k) * SCALE + gqc_ref[:, cols]).astype(BF)
        gk_ref[:, cols] = dot_tn(ds, q) * SCALE
        gv_ref[:, cols] = dot_tn(p.astype(BF), datt)


def finish_kernel(gk_ref, gv_ref, r1, r2, r3, r4, dk_ref, dv_ref, bufs):
    for h in range(gk_ref.shape[1] // HDIM):
        cols = slice(h * HDIM, (h + 1) * HDIM)
        for which, (g0_ref, out_ref) in enumerate(((gk_ref, dk_ref), (gv_ref, dv_ref))):
            g = None
            for ref, rows in ((r4, 16), (r3, 32), (r2, 64), (r1, 128)):
                own = ref[which * rows : (which + 1) * rows, cols].astype(F32)
                g = own if g is None else own + rep2(bufs.at[2 * h + which], 0.5 * g)
            g = g0_ref[:, cols] + rep2(bufs.at[2 * h + which], 0.5 * g)
            out_ref[:, cols] = g.astype(BF)


def shape(rows, cols, dtype=BF):
    return jax.ShapeDtypeStruct((rows, cols), dtype)


SMEM = pl.BlockSpec(memory_space=pltpu.SMEM)


def by_heads(rows, step):
    return pl.BlockSpec((rows, step), lambda i: (0, i))


def whole(rows, cols):
    return pl.BlockSpec((rows, cols), lambda i: (0, 0))


def call(kernel, out, **kw):
    return pl.pallas_call(kernel, out_shape=out, compiler_params=VMEM, **kw)


def per_device(queries, keys, values, d_out, w_out):
    q, k, v, dout = queries[0], keys[0], values[0], d_out[0]
    seq, dp = lax.axis_index("seq"), lax.axis_index("dp")
    place = jnp.stack([seq // 4, seq // 2 % 2, seq % 2, dp % 4]).astype(jnp.int32)
    step = 2 * HDIM
    grid = (WIDTH // step,)
    hs = functools.partial(by_heads, step=step)

    l1, l2, l3, l4 = call(
        coarsen_kernel,
        [shape(2 * rows, WIDTH) for rows in LEVEL_ROWS],
    )(k, v)
    a1 = swap(l1, "seq", CORE)
    b2 = swap(l2, "seq", ZLO)
    b4 = swap(l4, "seq", Y3)
    b3 = swap(l3, "seq", Y1)
    c4 = swap(b4, "seq", Y1)
    t = jnp.concatenate([b3, c4, b4])
    d = swap(t, "seq", ZLO)
    u = jnp.concatenate([b2, t, d])
    e = swap(u, "seq", CORE)

    own_t, other_t = call(
        arrange_kernel,
        [shape(1024, ROWS)] * 2,
        in_specs=[SMEM, pl.BlockSpec(memory_space=pltpu.VMEM)],
    )(place, dout)
    rec_t = swap(other_t, "seq", CORE)

    datt, qc, n0, m0, l0 = call(
        local_kernel,
        [shape(ROWS, WIDTH), shape(COARSE, WIDTH)] + [shape(ROWS, WIDTH, F32)] * 3,
        grid=grid,
        in_specs=[hs(ROWS)] * 3 + [whole(ROWS, DMODEL), hs(DMODEL)],
        out_specs=[hs(ROWS), hs(COARSE)] + [hs(ROWS)] * 3,
    )(q, k, v, dout, w_out)

    att, lse, w, f, c = call(
        forward_kernel,
        [
            shape(ROWS, WIDTH),
            shape(ROWS, WIDTH, F32),
            shape(COARSE, WIDTH, F32),
            shape(480, WIDTH, F32),
            shape(224, WIDTH, F32),
        ],
        grid=grid,
        in_specs=[hs(COARSE), hs(256), hs(384), hs(384)] + [hs(ROWS)] * 3,
        out_specs=[hs(ROWS), hs(ROWS), hs(COARSE), hs(480), hs(224)],
        scratch_shapes=[pltpu.VMEM((6, ROWS, HDIM), F32)],
    )(qc, a1, u, e, n0, m0, l0)

    attp = swap(att, "seq", CORE)

    send, keep, gqc = call(
        coarse_back_kernel,
        [shape(640, WIDTH), shape(384, WIDTH, F32), shape(ROWS, WIDTH, F32)],
        grid=grid,
        in_specs=[hs(COARSE), hs(256), hs(384), hs(384), hs(ROWS), hs(ROWS)]
        + [hs(COARSE), hs(480), hs(224)],
        out_specs=[hs(640), hs(384), hs(ROWS)],
        scratch_shapes=[pltpu.VMEM((4, ROWS, HDIM), F32)],
    )(qc, a1, u, e, datt, att, w, f, c)

    o = call(
        weight_kernel,
        [shape(256, 512)] * 4 + [shape(1024, 128)] * 4,
        in_specs=[SMEM] + [pl.BlockSpec(memory_space=pltpu.VMEM)] * 4,
    )(place, own_t, rec_t, att, attp)
    first = [
        o[0], swap(o[1], "seq", Y1), swap(o[2], "seq", Y2), swap(o[3], "seq", Y3),
        o[4], swap(o[5], "dp", X1), swap(o[6], "dp", X2), swap(o[7], "dp", X3),
    ]

    rc = swap(send, "seq", CORE)
    dq, gk0, gv0 = call(
        local_back_kernel,
        [shape(ROWS, WIDTH), shape(ROWS, WIDTH, F32), shape(ROWS, WIDTH, F32)],
        grid=grid,
        in_specs=[hs(ROWS)] * 7,
        out_specs=[hs(ROWS)] * 3,
    )(q, k, v, datt, att, lse, gqc)
    s = keep + rc[256:640].astype(F32)
    rz = swap(s[256:384].astype(BF), "seq", ZLO)
    r2 = swap(s[0:128].astype(BF), "seq", ZLO)
    t = s[128:256] + rz.astype(F32)
    ry = swap(t[0:96].astype(BF), "seq", Y1)
    r4 = swap((t[96:128] + ry[64:96].astype(F32)).astype(BF), "seq", Y3)
    dk, dv = call(
        finish_kernel,
        [shape(ROWS, WIDTH)] * 2,
        grid=grid,
        in_specs=[hs(ROWS)] * 2 + [hs(256), hs(128), hs(64), hs(32)],
        out_specs=[hs(ROWS)] * 2,
        scratch_shapes=[pltpu.VMEM((4, ROWS, HDIM), F32)],
    )(gk0, gv0, rc[0:256], r2, ry[0:64], r4)

    p = call(sum_first_kernel, [shape(256, 128)] * 8)(*first)
    second = [
        p[0], swap(p[1], "dp", X1), swap(p[2], "dp", X2), swap(p[3], "dp", X3),
        p[4], swap(p[5], "seq", Y1), swap(p[6], "seq", Y2), swap(p[7], "seq", Y3),
    ]
    kept, sent = call(sum_second_kernel, [shape(128, 256)] * 2)(*second)
    g = kept.astype(F32) + swap(sent, "seq", ZLO).astype(F32)
    for mask in (ZH1, ZH3):
        g = g.astype(BF)
        g = g.astype(F32) + swap(g, "dp", mask).astype(F32)
    g = g.astype(BF)
    dw = call(
        place_kernel,
        shape(128, WIDTH, F32),
        in_specs=[SMEM] + [pl.BlockSpec(memory_space=pltpu.VMEM)] * 4,
    )(place, g, swap(g, "dp", X1), swap(g, "dp", X2), swap(g, "dp", X3))
    return dq[None], dk[None], dv[None], dw


def solution(mesh):
    rows = P("dp", "seq", None)
    return jax.shard_map(
        per_device,
        mesh=mesh,
        in_specs=(rows, rows, rows, rows, P()),
        out_specs=(rows, rows, rows, P("seq", None)),
        check_vma=False,
    )
```

```python
import functools
import math

import jax
import jax.numpy as jnp
from jax import lax
from jax.experimental import pallas as pl
from jax.experimental.pallas import tpu as pltpu
from jax.sharding import PartitionSpec as P

HEADS = 8
HDIM = 128
ROWS = 256
WIDTH = 1024
DMODEL = 2048
SCALE = HDIM**-0.5
SCALE2 = SCALE * math.log2(math.e)
LEVEL_ROWS = (128, 64, 32, 16)
SPANS = {2: ((0, 64),), 3: ((128, 32), (256, 32)), 4: ((192, 16), (224, 16), (320, 16), (352, 16))}
BF = jnp.bfloat16
F32 = jnp.float32
VMEM = pltpu.CompilerParams(vmem_limit_bytes=16 * 1024 * 1024)

CORE, ZLO, Y1, Y2, Y3 = 1, 2, 4, 8, 12
X1, X2, X3, ZH1, ZH3 = 1, 2, 3, 4, 12
ORDER = (0, 3, 1, 2)


def swap(value, axis, mask):
    pairs = [(source, source ^ mask) for source in range(16)]
    return lax.ppermute(value, axis, pairs)


def dot(a, b):
    return jnp.dot(a, b, preferred_element_type=F32)


def dot_nt(a, b):
    return lax.dot_general(a, b, (((1,), (1,)), ((), ())), preferred_element_type=F32)


def dot_tn(a, b):
    return lax.dot_general(a, b, (((0,), (0,)), ((), ())), preferred_element_type=F32)


def pool_matrix(rows):
    r = lax.broadcasted_iota(jnp.int32, (rows, 2 * rows), 0)
    c = lax.broadcasted_iota(jnp.int32, (rows, 2 * rows), 1)
    return jnp.where((c == 2 * r) | (c == 2 * r + 1), 0.5, 0.0).astype(BF)


def coarse_levels(x):
    levels = []
    for rows in LEVEL_ROWS:
        x = dot(pool_matrix(rows), x).astype(BF)
        levels.append(x)
    return levels


def spread_matrix(rows):
    t = lax.broadcasted_iota(jnp.int32, (ROWS, rows), 0)
    r = lax.broadcasted_iota(jnp.int32, (ROWS, rows), 1)
    return jnp.where(t // (ROWS // rows) == r, 1.0, 0.0).astype(BF)


def average_matrix(level):
    a = lax.broadcasted_iota(jnp.int32, (ROWS, ROWS), 0)
    b = lax.broadcasted_iota(jnp.int32, (ROWS, ROWS), 1)
    return jnp.where(a // 2**level == b // 2**level, 2.0**-level, 0.0).astype(BF)


def rep2(buf, x):
    rows, cols = x.shape
    buf[pl.ds(0, rows, stride=2), 0:cols] = x
    buf[pl.ds(1, rows, stride=2), 0:cols] = x
    return buf[0 : 2 * rows, 0:cols]


def wide(column):
    return jnp.broadcast_to(column, (column.shape[0], HDIM))


def coarsen_kernel(k_ref, v_ref, o1, o2, o3, o4):
    ks = coarse_levels(k_ref[...])
    vs = coarse_levels(v_ref[...])
    for out, rows, k, v in zip((o1, o2, o3, o4), LEVEL_ROWS, ks, vs):
        out[0:rows, :] = k
        out[rows : 2 * rows, :] = v


def arrange_kernel(at_ref, dout_ref, own_ref, other_ref):
    y, zl, c = at_ref[0], at_ref[1], at_ref[2]
    for n in range(8):
        jy, iz = ORDER[n // 2], n % 2
        base = (y ^ jy) * 4 + (zl ^ iz) * 2
        for ref, core in ((own_ref, c), (other_ref, 1 - c)):
            at = pl.multiple_of((base + core) * 128, 128)
            block = dout_ref[:, pl.ds(at, 128)]
            ref[n * 128 : (n + 1) * 128, :] = block.T


def project_kernel(dout_ref, w_ref, datt_ref):
    datt_ref[...] = dot(dout_ref[...], w_ref[...]).astype(BF)


def local_kernel(q_ref, k_ref, v_ref, a_ref, qx_ref, n_ref, m_ref, l_ref):
    for n, x in enumerate(coarse_levels(q_ref[...])):
        qx_ref[n * ROWS : (n + 1) * ROWS, :] = dot(spread_matrix(x.shape[0]), x).astype(BF)
    for h in range(q_ref.shape[1] // HDIM):
        cols = slice(h * HDIM, (h + 1) * HDIM)
        s = jnp.concatenate(
            [
                dot_nt(q_ref[:, cols], k_ref[:, cols]) * SCALE2,
                dot_nt(qx_ref[0:ROWS, cols], a_ref[0:128, cols]) * SCALE2 + 1.0,
            ],
            axis=1,
        )
        m = jnp.max(s, axis=1, keepdims=True)
        e = jnp.exp2(s - m)
        l_ref[:, cols] = wide(jnp.sum(e, axis=1, keepdims=True))
        m_ref[:, cols] = wide(m)
        v = jnp.concatenate([v_ref[:, cols], a_ref[128:256, cols]], axis=0)
        n_ref[:, cols] = dot(e.astype(BF), v)


def sibling(level, a_ref, u_ref, e_ref, cols):
    if level == 1:
        return a_ref[0:128, cols], a_ref[128:256, cols]
    keys = [ref[at : at + n, cols] for ref in (u_ref, e_ref) for at, n in SPANS[level]]
    vals = [ref[at + n : at + 2 * n, cols] for ref in (u_ref, e_ref) for at, n in SPANS[level]]
    return jnp.concatenate(keys, axis=0), jnp.concatenate(vals, axis=0)


def forward_kernel(qx_ref, u_ref, e_ref, n_ref, m_ref, l_ref, att_ref, lse_ref):
    for h in range(qx_ref.shape[1] // HDIM):
        cols = slice(h * HDIM, (h + 1) * HDIM)
        scores, vals = [], []
        for level in range(2, 5):
            k, v = sibling(level, None, u_ref, e_ref, cols)
            q = qx_ref[(level - 1) * ROWS : level * ROWS, cols]
            scores.append(dot_nt(q, k) * SCALE2 + float(level))
            vals.append(v)
        s = jnp.concatenate(scores, axis=1)
        m0 = m_ref[:, cols]
        top = jnp.maximum(m0, wide(jnp.max(s, axis=1, keepdims=True)))
        e = jnp.exp2(s - jnp.concatenate([top] * 3, axis=1))
        own = jnp.exp2(m0 - top)
        total = own * l_ref[:, cols] + wide(jnp.sum(e, axis=1, keepdims=True))
        num = own * n_ref[:, cols] + dot(e.astype(BF), jnp.concatenate(vals, axis=0))
        att_ref[:, cols] = (num / total).astype(BF)
        lse_ref[:, cols] = top + jnp.log2(total)


def back_kernel(
    q_ref, k_ref, v_ref, qx_ref, a_ref, u_ref, e_ref, datt_ref, att_ref, lse_ref,
    send_ref, keep_ref, dq_ref, gk_ref, gv_ref, avg_ref,
):
    @pl.when(pl.program_id(0) == 0)
    def _():
        for level in range(1, 5):
            avg_ref[(level - 1) * ROWS : level * ROWS, :] = average_matrix(level)

    all_keys, all_ds = [], []
    for h in range(q_ref.shape[1] // HDIM):
        cols = slice(h * HDIM, (h + 1) * HDIM)
        datt = datt_ref[:, cols]
        delta = jnp.sum(datt.astype(F32) * att_ref[:, cols].astype(F32), axis=1, keepdims=True)
        delta = wide(delta).T[0:1, :]
        lse = lse_ref[:, cols].T[0:1, :]
        sides = [sibling(level, a_ref, u_ref, e_ref, cols) for level in range(1, 5)]
        queries = [qx_ref[n * ROWS : (n + 1) * ROWS, cols] for n in range(4)] + [q_ref[:, cols]]
        keys = [k for k, _ in sides] + [k_ref[:, cols]]
        vals = jnp.concatenate([v for _, v in sides] + [v_ref[:, cols]], axis=0)
        scores = [
            dot_nt(k, q) * SCALE2 + bias
            for k, q, bias in zip(keys, queries, (1.0, 2.0, 3.0, 4.0, 0.0))
        ]
        p = jnp.exp2(jnp.concatenate(scores, axis=0) - lse)
        ds = (p * (dot_nt(vals, datt) - delta)).astype(BF)
        gv = dot(p.astype(BF), datt)
        ds = [ds[n * 128 : (n + 1) * 128] for n in range(4)] + [ds[512:768]]
        all_keys.append(jnp.concatenate(keys, axis=0).T)
        all_ds.append(ds)
        for level in range(1, 5):
            gk_l = dot(ds[level - 1], queries[level - 1]) * SCALE
            gv_l = gv[(level - 1) * 128 : level * 128]
            if level == 1:
                send_ref[0:128, cols] = gk_l.astype(BF)
                send_ref[128:256, cols] = gv_l.astype(BF)
            else:
                row = 0
                for ref, off in ((keep_ref, 0), (send_ref, 256)):
                    for start, n in SPANS[level]:
                        to = off + start
                        ref[to : to + n, cols] = gk_l[row : row + n].astype(ref.dtype)
                        ref[to + n : to + 2 * n, cols] = gv_l[row : row + n].astype(ref.dtype)
                        row += n
        gk_ref[:, cols] = dot(ds[4], queries[4]) * SCALE
        gv_ref[:, cols] = gv[512:768]
    means = []
    for n in range(4):
        stacked = jnp.concatenate([ds[n] for ds in all_ds], axis=0)
        means.append(dot(stacked, avg_ref[n * ROWS : (n + 1) * ROWS, :]).astype(BF))
    for h in range(q_ref.shape[1] // HDIM):
        rows = slice(h * 128, (h + 1) * 128)
        ds = jnp.concatenate([m[rows] for m in means] + [all_ds[h][4]], axis=0)
        gq = dot(all_keys[h], ds)
        dq_ref[:, h * HDIM : (h + 1) * HDIM] = (gq.T * SCALE).astype(BF)


def weight_kernel(at_ref, own_ref, other_ref, att_ref, attp_ref, *outs):
    x = at_ref[3]

    def heads(ref, half):
        blocks = []
        for jx in ORDER:
            col = pl.multiple_of(((x ^ jx) * 2 + half) * 128, 128)
            blocks.append(ref[:, pl.ds(col, 128)])
        return jnp.concatenate(blocks, axis=1)

    def term(n, half):
        rows = slice(n * 256, (n + 1) * 256)
        return (dot(own_ref[rows, :], mine[half]) + dot(other_ref[rows, :], theirs[half])).astype(BF)

    mine = [heads(att_ref, half) for half in range(2)]
    theirs = [heads(attp_ref, half) for half in range(2)]
    for n in range(4):
        outs[n][...] = term(n, 0)
        part = term(n, 1)
        for m in range(4):
            outs[4 + m][n * 256 : (n + 1) * 256, :] = part[:, m * 128 : (m + 1) * 128]


def sum_first_kernel(*refs):
    ins, (keep_x, send_x, keep_y, send_y) = refs[:8], refs[8:]
    for n, out in enumerate((keep_x, send_x)):
        cols = slice(n * 256, (n + 1) * 256)
        out[...] = sum(r[:, cols].astype(F32) for r in ins[:4]).astype(out.dtype)
    for n, out in enumerate((keep_y, send_y)):
        rows = slice(n * 512, (n + 1) * 512)
        out[...] = sum(r[rows, :].astype(F32) for r in ins[4:]).astype(out.dtype)


def sum_second_kernel(in_x, got_x, in_y, got_y, keep_x, send_x, keep_y, send_y):
    for n, out in enumerate((keep_x, send_x)):
        cols = slice(n * 128, (n + 1) * 128)
        out[...] = (in_x[:, cols] + got_x[:, cols].astype(F32)).astype(out.dtype)
    for n, out in enumerate((keep_y, send_y)):
        rows = slice(n * 256, (n + 1) * 256)
        out[...] = (in_y[rows, :] + got_y[rows, :].astype(F32)).astype(out.dtype)


def sum_third_kernel(in_x, got_x, in_y, got_y, keep_ref, send_ref):
    for half, (own, got) in enumerate(((in_x, got_x), (in_y, got_y))):
        cols = slice(half * 128, (half + 1) * 128)
        total = own[...] + got[...].astype(F32)
        keep_ref[:, cols] = total[0:128]
        send_ref[:, cols] = total[128:256].astype(BF)


def place_kernel(at_ref, a, b, c, d, out_ref):
    x = at_ref[3]
    for j, ref in enumerate((a, b, c, d)):
        col = pl.multiple_of((x ^ j) * 256, 256)
        out_ref[:, pl.ds(col, 256)] = ref[...].astype(F32)


def finish_kernel(gk_ref, gv_ref, r1, r2, r3, r4, dk_ref, dv_ref, bufs):
    for h in range(gk_ref.shape[1] // HDIM):
        cols = slice(h * HDIM, (h + 1) * HDIM)
        for which, (g0_ref, out_ref) in enumerate(((gk_ref, dk_ref), (gv_ref, dv_ref))):
            g = None
            for ref, rows in ((r4, 16), (r3, 32), (r2, 64), (r1, 128)):
                own = ref[which * rows : (which + 1) * rows, cols].astype(F32)
                g = own if g is None else own + rep2(bufs.at[2 * h + which], 0.5 * g)
            g = g0_ref[:, cols] + rep2(bufs.at[2 * h + which], 0.5 * g)
            out_ref[:, cols] = g.astype(BF)


def shape(rows, cols, dtype=BF):
    return jax.ShapeDtypeStruct((rows, cols), dtype)


SMEM = pl.BlockSpec(memory_space=pltpu.SMEM)


def by_heads(rows, step):
    return pl.BlockSpec((rows, step), lambda i: (0, i))


def whole(rows, cols):
    return pl.BlockSpec((rows, cols), lambda i: (0, 0))


def cost(flops, bytes_accessed):
    return pl.CostEstimate(flops=int(flops), bytes_accessed=int(bytes_accessed), transcendentals=0)


def call(kernel, out, **kw):
    return pl.pallas_call(kernel, out_shape=out, compiler_params=VMEM, **kw)


def per_device(queries, keys, values, d_out, w_out):
    q, k, v, dout = queries[0], keys[0], values[0], d_out[0]
    seq, dp = lax.axis_index("seq"), lax.axis_index("dp")
    place = jnp.stack([seq // 4, seq // 2 % 2, seq % 2, dp % 4]).astype(jnp.int32)
    step = 2 * HDIM
    grid = (WIDTH // step,)
    hs = functools.partial(by_heads, step=step)

    l1, l2, l3, l4 = call(
        coarsen_kernel,
        [shape(2 * rows, WIDTH) for rows in LEVEL_ROWS],
    )(k, v)
    b4 = swap(l4, "seq", Y3)
    c4 = swap(l4, "seq", Y2)
    b3 = swap(l3, "seq", Y1)
    b2 = swap(l2, "seq", ZLO)
    a1 = swap(l1, "seq", CORE)
    qx, n0, m0, l0 = call(
        local_kernel,
        [shape(4 * ROWS, WIDTH)] + [shape(ROWS, WIDTH, F32)] * 3,
        grid=grid,
        in_specs=[hs(ROWS)] * 3 + [hs(256)],
        out_specs=[hs(4 * ROWS)] + [hs(ROWS)] * 3,
        cost_estimate=cost(2.0e9, 10e6),
    )(q, k, v, a1)
    t = jnp.concatenate([b3, c4, b4])
    t, n0 = lax.optimization_barrier((t, n0))
    d = swap(t, "seq", ZLO)
    datt = call(
        project_kernel,
        shape(ROWS, WIDTH),
        grid=grid,
        in_specs=[whole(ROWS, DMODEL), hs(DMODEL)],
        out_specs=hs(ROWS),
        cost_estimate=cost(2.0e9, 10e6),
    )(dout, w_out)
    u = jnp.concatenate([b2, t, d])
    u, datt = lax.optimization_barrier((u, datt))
    e = swap(u, "seq", CORE)
    own_t, other_t = call(
        arrange_kernel,
        [shape(1024, ROWS)] * 2,
        in_specs=[SMEM, pl.BlockSpec(memory_space=pltpu.VMEM)],
    )(place, dout)
    rec_t = swap(other_t, "seq", CORE)
    att, lse = call(
        forward_kernel,
        [shape(ROWS, WIDTH), shape(ROWS, WIDTH, F32)],
        grid=grid,
        in_specs=[hs(4 * ROWS), hs(384), hs(384)] + [hs(ROWS)] * 3,
        out_specs=[hs(ROWS), hs(ROWS)],
        cost_estimate=cost(1.0e9, 8e6),
    )(qx, u, e, n0, m0, l0)

    attp = swap(att, "seq", CORE)
    o = call(
        weight_kernel,
        [shape(256, 512)] * 4 + [shape(1024, 128)] * 4,
        in_specs=[SMEM] + [pl.BlockSpec(memory_space=pltpu.VMEM)] * 4,
        cost_estimate=cost(1.0e9, 4e6),
    )(place, own_t, rec_t, att, attp)
    keep_x, send_x, keep_y, send_y = call(
        sum_first_kernel,
        [shape(256, 256, F32), shape(256, 256), shape(512, 128, F32), shape(512, 128)],
    )(
        o[0], swap(o[1], "seq", Y3), swap(o[2], "seq", Y1), swap(o[3], "seq", Y2),
        o[4], swap(o[5], "dp", X3), swap(o[6], "dp", X1), swap(o[7], "dp", X2),
    )
    send, keep, dq, gk0, gv0 = call(
        back_kernel,
        [shape(640, WIDTH), shape(384, WIDTH, F32), shape(ROWS, WIDTH)]
        + [shape(ROWS, WIDTH, F32)] * 2,
        grid=grid,
        in_specs=[hs(ROWS)] * 3 + [hs(4 * ROWS), hs(256), hs(384), hs(384)] + [hs(ROWS)] * 3,
        out_specs=[hs(640), hs(384)] + [hs(ROWS)] * 3,
        scratch_shapes=[pltpu.VMEM((4 * ROWS, ROWS), BF)],
        cost_estimate=cost(4.0e9, 12e6),
    )(q, k, v, qx, a1, u, e, datt, att, lse)
    send, _ = lax.optimization_barrier((send, send_x))

    rc = swap(send, "seq", CORE)
    s = keep + rc[256:640].astype(F32)
    rz = swap(s[256:384].astype(BF), "seq", ZLO)
    r2 = swap(s[0:128].astype(BF), "seq", ZLO)
    t = s[128:256] + rz.astype(F32)
    ry = swap(t[0:96].astype(BF), "seq", Y1)
    r4 = swap((t[96:128] + ry[64:96].astype(F32)).astype(BF), "seq", Y3)
    dk, dv = call(
        finish_kernel,
        [shape(ROWS, WIDTH)] * 2,
        grid=grid,
        in_specs=[hs(ROWS)] * 2 + [hs(256), hs(128), hs(64), hs(32)],
        out_specs=[hs(ROWS)] * 2,
        scratch_shapes=[pltpu.VMEM((4, ROWS, HDIM), F32)],
    )(gk0, gv0, rc, r2, ry, r4)

    halves = [shape(256, 128, F32), shape(256, 128)] * 2
    keep_x, send_x, keep_y, send_y = call(sum_second_kernel, halves)(
        keep_x, swap(send_x, "dp", X1), keep_y, swap(send_y, "seq", Y1)
    )
    kept, sent = call(sum_third_kernel, [shape(128, 256, F32), shape(128, 256)])(
        keep_x, swap(send_x, "dp", X3), keep_y, swap(send_y, "seq", Y3)
    )
    g = kept + swap(sent, "seq", ZLO).astype(F32)
    for mask in (ZH1, ZH3):
        g = g.astype(BF)
        g = g.astype(F32) + swap(g, "dp", mask).astype(F32)
    g = g.astype(BF)
    dw = call(
        place_kernel,
        shape(128, WIDTH, F32),
        in_specs=[SMEM] + [pl.BlockSpec(memory_space=pltpu.VMEM)] * 4,
    )(place, g, swap(g, "dp", X1), swap(g, "dp", X2), swap(g, "dp", X3))
    return dq[None], dk[None], dv[None], dw


def solution(mesh):
    rows = P("dp", "seq", None)
    return jax.shard_map(
        per_device,
        mesh=mesh,
        in_specs=(rows, rows, rows, rows, P()),
        out_specs=(rows, rows, rows, P("seq", None)),
        check_vma=False,
    )
```

```python
import functools
import math

import jax
import jax.numpy as jnp
from jax import lax
from jax.experimental import pallas as pl
from jax.experimental.pallas import tpu as pltpu
from jax.sharding import PartitionSpec as P

HEADS = 8
HDIM = 128
ROWS = 256
WIDTH = 1024
DMODEL = 2048
SCALE = HDIM**-0.5
SCALE2 = SCALE * math.log2(math.e)
LEVEL_ROWS = (128, 64, 32, 16)
SPANS = {2: ((0, 64),), 3: ((128, 32), (256, 32)), 4: ((192, 16), (224, 16), (320, 16), (352, 16))}
BF = jnp.bfloat16
F32 = jnp.float32
VMEM = pltpu.CompilerParams(vmem_limit_bytes=16 * 1024 * 1024)

CORE, ZLO, Y1, Y2, Y3 = 1, 2, 4, 8, 12
X1, X2, X3, ZH1, ZH3 = 1, 2, 3, 4, 12
ORDER = (0, 3, 1, 2)


def swap(value, axis, mask):
    pairs = [(source, source ^ mask) for source in range(16)]
    return lax.ppermute(value, axis, pairs)


def dot(a, b):
    return jnp.dot(a, b, preferred_element_type=F32)


def dot_nt(a, b):
    return lax.dot_general(a, b, (((1,), (1,)), ((), ())), preferred_element_type=F32)


def dot_tn(a, b):
    return lax.dot_general(a, b, (((0,), (0,)), ((), ())), preferred_element_type=F32)


def pool_matrix(rows):
    r = lax.broadcasted_iota(jnp.int32, (rows, 2 * rows), 0)
    c = lax.broadcasted_iota(jnp.int32, (rows, 2 * rows), 1)
    return jnp.where((c == 2 * r) | (c == 2 * r + 1), 0.5, 0.0).astype(BF)


def coarse_levels(x):
    levels = []
    for rows in LEVEL_ROWS:
        x = dot(pool_matrix(rows), x).astype(BF)
        levels.append(x)
    return levels


def spread_matrix(rows):
    t = lax.broadcasted_iota(jnp.int32, (ROWS, rows), 0)
    r = lax.broadcasted_iota(jnp.int32, (ROWS, rows), 1)
    return jnp.where(t // (ROWS // rows) == r, 1.0, 0.0).astype(BF)


def average_matrix(level):
    a = lax.broadcasted_iota(jnp.int32, (ROWS, ROWS), 0)
    b = lax.broadcasted_iota(jnp.int32, (ROWS, ROWS), 1)
    return jnp.where(a // 2**level == b // 2**level, 2.0**-level, 0.0).astype(BF)


def rep2(buf, x):
    rows, cols = x.shape
    buf[pl.ds(0, rows, stride=2), 0:cols] = x
    buf[pl.ds(1, rows, stride=2), 0:cols] = x
    return buf[0 : 2 * rows, 0:cols]


def wide(column):
    return jnp.broadcast_to(column, (column.shape[0], HDIM))


def coarsen_kernel(k_ref, v_ref, o1, o2, o3, o4):
    ks = coarse_levels(k_ref[...])
    vs = coarse_levels(v_ref[...])
    for out, rows, k, v in zip((o1, o2, o3, o4), LEVEL_ROWS, ks, vs):
        out[0:rows, :] = k
        out[rows : 2 * rows, :] = v


def arrange_kernel(dout_ref, own_ref, other_ref):
    seq = lax.axis_index("seq")
    y, zl, c = seq >> 2, (seq >> 1) & 1, seq & 1
    for n in range(8):
        jy, iz = ORDER[n // 2], n % 2
        base = (y ^ jy) * 4 + (zl ^ iz) * 2
        for ref, core in ((own_ref, c), (other_ref, 1 - c)):
            at = pl.multiple_of((base + core) * 128, 128)
            block = dout_ref[:, pl.ds(at, 128)]
            ref[n * 128 : (n + 1) * 128, :] = block.T


def project_kernel(dout_ref, w_ref, datt_ref):
    datt_ref[...] = dot(dout_ref[...], w_ref[...]).astype(BF)


def local_kernel(q_ref, k_ref, v_ref, a_ref, qx_ref, n_ref, m_ref, l_ref):
    for n, x in enumerate(coarse_levels(q_ref[...])):
        qx_ref[n * ROWS : (n + 1) * ROWS, :] = dot(spread_matrix(x.shape[0]), x).astype(BF)
    for h in range(q_ref.shape[1] // HDIM):
        cols = slice(h * HDIM, (h + 1) * HDIM)
        s = jnp.concatenate(
            [
                dot_nt(q_ref[:, cols], k_ref[:, cols]) * SCALE2,
                dot_nt(qx_ref[0:ROWS, cols], a_ref[0:128, cols]) * SCALE2 + 1.0,
            ],
            axis=1,
        )
        m = jnp.max(s, axis=1, keepdims=True)
        e = jnp.exp2(s - m)
        l_ref[:, cols] = wide(jnp.sum(e, axis=1, keepdims=True))
        m_ref[:, cols] = wide(m)
        v = jnp.concatenate([v_ref[:, cols], a_ref[128:256, cols]], axis=0)
        n_ref[:, cols] = dot(e.astype(BF), v)


def sibling(level, a_ref, u_ref, e_ref, cols):
    if level == 1:
        return a_ref[0:128, cols], a_ref[128:256, cols]
    keys = [ref[at : at + n, cols] for ref in (u_ref, e_ref) for at, n in SPANS[level]]
    vals = [ref[at + n : at + 2 * n, cols] for ref in (u_ref, e_ref) for at, n in SPANS[level]]
    return jnp.concatenate(keys, axis=0), jnp.concatenate(vals, axis=0)


def forward_kernel(qx_ref, u_ref, e_ref, n_ref, m_ref, l_ref, att_ref, lse_ref):
    for h in range(qx_ref.shape[1] // HDIM):
        cols = slice(h * HDIM, (h + 1) * HDIM)
        scores, vals = [], []
        for level in range(2, 5):
            k, v = sibling(level, None, u_ref, e_ref, cols)
            q = qx_ref[(level - 1) * ROWS : level * ROWS, cols]
            scores.append(dot_nt(q, k) * SCALE2 + float(level))
            vals.append(v)
        s = jnp.concatenate(scores, axis=1)
        m0 = m_ref[:, cols]
        top = jnp.maximum(m0, wide(jnp.max(s, axis=1, keepdims=True)))
        e = jnp.exp2(s - jnp.concatenate([top] * 3, axis=1))
        own = jnp.exp2(m0 - top)
        total = own * l_ref[:, cols] + wide(jnp.sum(e, axis=1, keepdims=True))
        num = own * n_ref[:, cols] + dot(e.astype(BF), jnp.concatenate(vals, axis=0))
        att_ref[:, cols] = (num / total).astype(BF)
        lse_ref[:, cols] = top + jnp.log2(total)


def row_form(datt_ref, att_ref, lse_ref, cols):
    datt = datt_ref[:, cols].astype(F32)
    delta = jnp.sum(datt * att_ref[:, cols].astype(F32), axis=1, keepdims=True)
    return wide(delta).T[0:1, :], lse_ref[:, cols].T[0:1, :]


def back_kernel(
    qx_ref, a_ref, u_ref, e_ref, datt_ref, att_ref, lse_ref, send_ref, keep_ref, dq_ref, avg_ref
):
    @pl.when(pl.program_id(0) == 0)
    def _():
        for level in range(1, 5):
            avg_ref[(level - 1) * ROWS : level * ROWS, :] = average_matrix(level)

    all_keys, all_ds = [], []
    for h in range(qx_ref.shape[1] // HDIM):
        cols = slice(h * HDIM, (h + 1) * HDIM)
        datt = datt_ref[:, cols]
        delta, lse = row_form(datt_ref, att_ref, lse_ref, cols)
        sides = [sibling(level, a_ref, u_ref, e_ref, cols) for level in range(1, 5)]
        queries = [qx_ref[n * ROWS : (n + 1) * ROWS, cols] for n in range(4)]
        keys = [k for k, _ in sides]
        vals = jnp.concatenate([v for _, v in sides], axis=0)
        scores = [dot_nt(keys[n], queries[n]) * SCALE2 + float(n + 1) for n in range(4)]
        p = jnp.exp2(jnp.concatenate(scores, axis=0) - lse)
        ds = (p * (dot_nt(vals, datt) - delta)).astype(BF)
        gv = dot(p.astype(BF), datt)
        ds = [ds[n * 128 : (n + 1) * 128] for n in range(4)]
        all_keys.append(jnp.concatenate(keys, axis=0).T)
        all_ds.append(ds)
        for level in range(1, 5):
            gk_l = dot(ds[level - 1], queries[level - 1]) * SCALE
            gv_l = gv[(level - 1) * 128 : level * 128]
            if level == 1:
                send_ref[0:128, cols] = gk_l.astype(BF)
                send_ref[128:256, cols] = gv_l.astype(BF)
            else:
                row = 0
                for ref, off in ((keep_ref, 0), (send_ref, 256)):
                    for start, n in SPANS[level]:
                        to = off + start
                        ref[to : to + n, cols] = gk_l[row : row + n].astype(ref.dtype)
                        ref[to + n : to + 2 * n, cols] = gv_l[row : row + n].astype(ref.dtype)
                        row += n
    means = []
    for n in range(4):
        stacked = jnp.concatenate([ds[n] for ds in all_ds], axis=0)
        means.append(dot(stacked, avg_ref[n * ROWS : (n + 1) * ROWS, :]).astype(BF))
    for h in range(qx_ref.shape[1] // HDIM):
        rows = slice(h * 128, (h + 1) * 128)
        gq = dot(all_keys[h], jnp.concatenate([m[rows] for m in means], axis=0))
        dq_ref[:, h * HDIM : (h + 1) * HDIM] = gq.T * SCALE


def local_back_kernel(
    q_ref, k_ref, v_ref, datt_ref, att_ref, lse_ref, gq_ref, dq_ref, gk_ref, gv_ref
):
    for h in range(q_ref.shape[1] // HDIM):
        cols = slice(h * HDIM, (h + 1) * HDIM)
        q, k, v, datt = q_ref[:, cols], k_ref[:, cols], v_ref[:, cols], datt_ref[:, cols]
        delta, lse = row_form(datt_ref, att_ref, lse_ref, cols)
        p = jnp.exp2(dot_nt(k, q) * SCALE2 - lse)
        ds = (p * (dot_nt(v, datt) - delta)).astype(BF)
        gk_ref[:, cols] = dot(ds, q) * SCALE
        gv_ref[:, cols] = dot(p.astype(BF), datt)
        gq = dot(k.T, ds)
        dq_ref[:, cols] = (gq_ref[:, cols] + gq.T * SCALE).astype(BF)


def weight_kernel(own_ref, other_ref, att_ref, attp_ref, *outs):
    x = lax.axis_index("dp") & 3

    def heads(ref, half):
        blocks = []
        for jx in ORDER:
            col = pl.multiple_of(((x ^ jx) * 2 + half) * 128, 128)
            blocks.append(ref[:, pl.ds(col, 128)])
        return jnp.concatenate(blocks, axis=1)

    def term(n, half):
        rows = slice(n * 256, (n + 1) * 256)
        return (dot(own_ref[rows, :], mine[half]) + dot(other_ref[rows, :], theirs[half])).astype(BF)

    mine = [heads(att_ref, half) for half in range(2)]
    theirs = [heads(attp_ref, half) for half in range(2)]
    for n in range(4):
        outs[n][...] = term(n, 0)
        part = term(n, 1)
        for m in range(4):
            outs[4 + m][n * 256 : (n + 1) * 256, :] = part[:, m * 128 : (m + 1) * 128]


def sum_first_kernel(*refs):
    ins, (keep_x, send_x, keep_y, send_y) = refs[:8], refs[8:]
    for n, out in enumerate((keep_x, send_x)):
        cols = slice(n * 256, (n + 1) * 256)
        out[...] = sum(r[:, cols].astype(F32) for r in ins[:4]).astype(out.dtype)
    for n, out in enumerate((keep_y, send_y)):
        rows = slice(n * 512, (n + 1) * 512)
        out[...] = sum(r[rows, :].astype(F32) for r in ins[4:]).astype(out.dtype)


def sum_second_kernel(in_x, got_x, in_y, got_y, keep_x, send_x, keep_y, send_y):
    for n, out in enumerate((keep_x, send_x)):
        cols = slice(n * 128, (n + 1) * 128)
        out[...] = (in_x[:, cols] + got_x[:, cols].astype(F32)).astype(out.dtype)
    for n, out in enumerate((keep_y, send_y)):
        rows = slice(n * 256, (n + 1) * 256)
        out[...] = (in_y[rows, :] + got_y[rows, :].astype(F32)).astype(out.dtype)


def sum_third_kernel(in_x, got_x, in_y, got_y, keep_ref, send_ref):
    for half, (own, got) in enumerate(((in_x, got_x), (in_y, got_y))):
        cols = slice(half * 128, (half + 1) * 128)
        total = own[...] + got[...].astype(F32)
        keep_ref[:, cols] = total[0:128]
        send_ref[:, cols] = total[128:256].astype(BF)


def place_kernel(a, b, c, d, out_ref):
    x = lax.axis_index("dp") & 3
    for j, ref in enumerate((a, b, c, d)):
        col = pl.multiple_of((x ^ j) * 256, 256)
        out_ref[:, pl.ds(col, 256)] = ref[...].astype(F32)


def add_first_kernel(keep_ref, got_ref, out_ref, rest_ref):
    out_ref[0:128, :] = (keep_ref[256:384, :] + got_ref[512:640, :].astype(F32)).astype(BF)
    out_ref[128:256, :] = (keep_ref[0:128, :] + got_ref[256:384, :].astype(F32)).astype(BF)
    rest_ref[...] = keep_ref[128:256, :] + got_ref[384:512, :].astype(F32)


def add_second_kernel(rest_ref, got_ref, send_ref, last_ref):
    total = rest_ref[...] + got_ref[0:128, :].astype(F32)
    send_ref[...] = total[0:96].astype(BF)
    last_ref[...] = total[96:128]


def add_third_kernel(last_ref, got_ref, out_ref):
    out_ref[...] = (last_ref[...] + got_ref[64:96, :].astype(F32)).astype(BF)


def finish_kernel(gk_ref, gv_ref, r1, r2, r3, r4, dk_ref, dv_ref, bufs):
    for h in range(gk_ref.shape[1] // HDIM):
        cols = slice(h * HDIM, (h + 1) * HDIM)
        for which, (g0_ref, out_ref) in enumerate(((gk_ref, dk_ref), (gv_ref, dv_ref))):
            g = None
            for ref, rows in ((r4, 16), (r3, 32), (r2, 64), (r1, 128)):
                own = ref[which * rows : (which + 1) * rows, cols].astype(F32)
                g = own if g is None else own + rep2(bufs.at[2 * h + which], 0.5 * g)
            g = g0_ref[:, cols] + rep2(bufs.at[2 * h + which], 0.5 * g)
            out_ref[:, cols] = g.astype(BF)


def shape(rows, cols, dtype=BF):
    return jax.ShapeDtypeStruct((rows, cols), dtype)


def by_heads(rows, step):
    return pl.BlockSpec((rows, step), lambda i: (0, i))


def whole(rows, cols):
    return pl.BlockSpec((rows, cols), lambda i: (0, 0))


def call(kernel, out, flops=1, moved=1, **kw):
    cost = pl.CostEstimate(flops=int(flops), bytes_accessed=int(moved), transcendentals=0)
    return pl.pallas_call(kernel, out_shape=out, compiler_params=VMEM, cost_estimate=cost, **kw)


def per_device(queries, keys, values, d_out, w_out):
    q, k, v, dout = queries[0], keys[0], values[0], d_out[0]
    step = 2 * HDIM
    grid = (WIDTH // step,)
    hs = functools.partial(by_heads, step=step)

    l1, l2, l3, l4 = call(
        coarsen_kernel,
        [shape(2 * rows, WIDTH) for rows in LEVEL_ROWS],
    )(k, v)
    b4 = swap(l4, "seq", Y3)
    c4 = swap(l4, "seq", Y2)
    b3 = swap(l3, "seq", Y1)
    b2 = swap(l2, "seq", ZLO)
    a1 = swap(l1, "seq", CORE)
    t = jnp.concatenate([b3, c4, b4])
    datt = call(
        project_kernel,
        shape(ROWS, WIDTH),
        grid=grid,
        in_specs=[whole(ROWS, DMODEL), hs(DMODEL)],
        out_specs=hs(ROWS),
    )(dout, w_out)
    t, datt = lax.optimization_barrier((t, datt))
    d = swap(t, "seq", ZLO)
    qx, n0, m0, l0 = call(
        local_kernel,
        flops=8e9,
        moved=20e6,
        out=[shape(4 * ROWS, WIDTH)] + [shape(ROWS, WIDTH, F32)] * 3,
        grid=grid,
        in_specs=[hs(ROWS)] * 3 + [hs(256)],
        out_specs=[hs(4 * ROWS)] + [hs(ROWS)] * 3,
    )(q, k, v, a1)
    b2, n0 = lax.optimization_barrier((b2, n0))
    u = jnp.concatenate([b2, t, d])
    e = swap(u, "seq", CORE)
    own_t, other_t = call(
        arrange_kernel,
        [shape(1024, ROWS)] * 2,
        in_specs=[pl.BlockSpec(memory_space=pltpu.VMEM)],
    )(dout)
    rec_t = swap(other_t, "seq", CORE)
    att, lse = call(
        forward_kernel,
        [shape(ROWS, WIDTH), shape(ROWS, WIDTH, F32)],
        grid=grid,
        in_specs=[hs(4 * ROWS), hs(384), hs(384)] + [hs(ROWS)] * 3,
        out_specs=[hs(ROWS), hs(ROWS)],
    )(qx, u, e, n0, m0, l0)

    attp = swap(att, "seq", CORE)
    o = call(
        weight_kernel,
        [shape(256, 512)] * 4 + [shape(1024, 128)] * 4,
        in_specs=[pl.BlockSpec(memory_space=pltpu.VMEM)] * 4,
    )(own_t, rec_t, att, attp)
    keep_x, send_x, keep_y, send_y = call(
        sum_first_kernel,
        [shape(256, 256, F32), shape(256, 256), shape(512, 128, F32), shape(512, 128)],
    )(
        o[0], swap(o[1], "seq", Y3), swap(o[2], "seq", Y1), swap(o[3], "seq", Y2),
        o[4], swap(o[5], "dp", X3), swap(o[6], "dp", X1), swap(o[7], "dp", X2),
    )
    send, keep, gq = call(
        back_kernel,
        [shape(640, WIDTH), shape(384, WIDTH, F32), shape(ROWS, WIDTH, F32)],
        grid=grid,
        in_specs=[hs(4 * ROWS), hs(256), hs(384), hs(384)] + [hs(ROWS)] * 3,
        out_specs=[hs(640), hs(384), hs(ROWS)],
        scratch_shapes=[pltpu.VMEM((4 * ROWS, ROWS), BF)],
    )(qx, a1, u, e, datt, att, lse)
    send, _ = lax.optimization_barrier((send, send_x))

    halves = [shape(256, 128, F32), shape(256, 128)] * 2
    keep_x, next_x, keep_y, next_y = call(sum_second_kernel, halves)(
        keep_x, swap(send_x, "dp", X1), keep_y, swap(send_y, "seq", Y1)
    )
    dq, gk0, gv0 = call(
        local_back_kernel,
        flops=5e9,
        moved=15e6,
        out=[shape(ROWS, WIDTH)] + [shape(ROWS, WIDTH, F32)] * 2,
        grid=grid,
        in_specs=[hs(ROWS)] * 7,
        out_specs=[hs(ROWS)] * 3,
    )(q, k, v, datt, att, lse, gq)
    next_x, gk0 = lax.optimization_barrier((next_x, gk0))

    rc = swap(send, "seq", CORE)
    keep, _ = lax.optimization_barrier((keep, next_x))
    out, rest = call(add_first_kernel, [shape(256, WIDTH), shape(128, WIDTH, F32)])(keep, rc)
    rz = swap(out, "seq", ZLO)
    ty, t4 = call(add_second_kernel, [shape(96, WIDTH), shape(32, WIDTH, F32)])(rest, rz)
    ry = swap(ty, "seq", Y1)
    r4 = call(add_third_kernel, shape(32, WIDTH))(t4, ry)

    kept, sent = call(sum_third_kernel, [shape(128, 256, F32), shape(128, 256)])(
        keep_x, swap(next_x, "dp", X3), keep_y, swap(next_y, "seq", Y3)
    )
    g = (kept + swap(sent, "seq", ZLO).astype(F32)).astype(BF)
    g = g.astype(F32) + swap(g, "dp", ZH1).astype(F32)
    g, r4 = lax.optimization_barrier((g.astype(BF), r4))
    r4 = swap(r4, "seq", Y3)
    g = (g.astype(F32) + swap(g, "dp", ZH3).astype(F32)).astype(BF)
    g, r4 = lax.optimization_barrier((g, r4))
    lower = pl.BlockSpec((128, step), lambda i: (1, i))
    dk, dv = call(
        finish_kernel,
        flops=3e9,
        moved=8e6,
        out=[shape(ROWS, WIDTH)] * 2,
        grid=grid,
        in_specs=[hs(ROWS)] * 2 + [hs(256), lower, hs(64), hs(32)],
        out_specs=[hs(ROWS)] * 2,
        scratch_shapes=[pltpu.VMEM((4, ROWS, HDIM), F32)],
    )(gk0, gv0, rc, rz, ry, r4)
    dw = call(
        place_kernel,
        shape(128, WIDTH, F32),
        in_specs=[pl.BlockSpec(memory_space=pltpu.VMEM)] * 4,
    )(g, swap(g, "dp", X1), swap(g, "dp", X2), swap(g, "dp", X3))
    return dq[None], dk[None], dv[None], dw


def solution(mesh):
    rows = P("dp", "seq", None)
    return jax.shard_map(
        per_device,
        mesh=mesh,
        in_specs=(rows, rows, rows, rows, P()),
        out_specs=(rows, rows, rows, P("seq", None)),
        check_vma=False,
    )
```

```python
import functools
import math

import jax
import jax.numpy as jnp
from jax import lax
from jax.experimental import pallas as pl
from jax.experimental.pallas import tpu as pltpu
from jax.sharding import PartitionSpec as P

HEADS = 8
HDIM = 128
ROWS = 256
WIDTH = 1024
DMODEL = 2048
SCALE = HDIM**-0.5
SCALE2 = SCALE * math.log2(math.e)
LEVEL_ROWS = (128, 64, 32, 16)
SPANS = {2: ((0, 64),), 3: ((128, 32), (256, 32)), 4: ((192, 16), (224, 16), (320, 16), (352, 16))}
BF = jnp.bfloat16
F32 = jnp.float32
VMEM = pltpu.CompilerParams(vmem_limit_bytes=16 * 1024 * 1024)

CORE, ZLO, Y1, Y2, Y3 = 1, 2, 4, 8, 12
X1, X2, X3, ZH1, ZH3 = 1, 2, 3, 4, 12
ORDER_X = (0, 3, 1, 2)
ORDER_Y = (0, 1, 3, 2)


def swap(value, axis, mask):
    pairs = [(source, source ^ mask) for source in range(16)]
    return lax.ppermute(value, axis, pairs)


def dot(a, b):
    return jnp.dot(a, b, preferred_element_type=F32)


def dot_nt(a, b):
    return lax.dot_general(a, b, (((1,), (1,)), ((), ())), preferred_element_type=F32)


def dot_tn(a, b):
    return lax.dot_general(a, b, (((0,), (0,)), ((), ())), preferred_element_type=F32)


def pool_matrix(rows):
    r = lax.broadcasted_iota(jnp.int32, (rows, 2 * rows), 0)
    c = lax.broadcasted_iota(jnp.int32, (rows, 2 * rows), 1)
    return jnp.where((c == 2 * r) | (c == 2 * r + 1), 0.5, 0.0).astype(BF)


def coarse_levels(x):
    levels = []
    for rows in LEVEL_ROWS:
        x = dot(pool_matrix(rows), x).astype(BF)
        levels.append(x)
    return levels


def spread_matrix(rows):
    t = lax.broadcasted_iota(jnp.int32, (ROWS, rows), 0)
    r = lax.broadcasted_iota(jnp.int32, (ROWS, rows), 1)
    return jnp.where(t // (ROWS // rows) == r, 1.0, 0.0).astype(BF)


def average_matrix(level):
    a = lax.broadcasted_iota(jnp.int32, (ROWS, ROWS), 0)
    b = lax.broadcasted_iota(jnp.int32, (ROWS, ROWS), 1)
    return jnp.where(a // 2**level == b // 2**level, 2.0**-level, 0.0).astype(BF)


def rep2(buf, x):
    rows, cols = x.shape
    buf[pl.ds(0, rows, stride=2), 0:cols] = x
    buf[pl.ds(1, rows, stride=2), 0:cols] = x
    return buf[0 : 2 * rows, 0:cols]


def wide(column):
    return jnp.broadcast_to(column, (column.shape[0], HDIM))


def coarsen_kernel(k_ref, v_ref, o1, o2, o3, o4):
    ks = coarse_levels(k_ref[...])
    vs = coarse_levels(v_ref[...])
    for out, rows, k, v in zip((o1, o2, o3, o4), LEVEL_ROWS, ks, vs):
        out[0:rows, :] = k
        out[rows : 2 * rows, :] = v


def arrange_kernel(dout_ref, own_ref, other_ref):
    seq = lax.axis_index("seq")
    y, zl, c = seq >> 2, (seq >> 1) & 1, seq & 1
    for n in range(8):
        jy, iz = ORDER_Y[n // 2], n % 2
        base = (y ^ jy) * 4 + (zl ^ iz) * 2
        for ref, core in ((own_ref, c), (other_ref, 1 - c)):
            at = pl.multiple_of((base + core) * 128, 128)
            block = dout_ref[:, pl.ds(at, 128)]
            ref[n * 128 : (n + 1) * 128, :] = block.T


def project_kernel(dout_ref, w_ref, datt_ref):
    datt_ref[...] = dot(dout_ref[...], w_ref[...]).astype(BF)


def local_kernel(q_ref, k_ref, v_ref, a_ref, qx_ref, n_ref, m_ref, l_ref):
    for n, x in enumerate(coarse_levels(q_ref[...])):
        qx_ref[n * ROWS : (n + 1) * ROWS, :] = dot(spread_matrix(x.shape[0]), x).astype(BF)
    for h in range(q_ref.shape[1] // HDIM):
        cols = slice(h * HDIM, (h + 1) * HDIM)
        s = jnp.concatenate(
            [
                dot_nt(q_ref[:, cols], k_ref[:, cols]) * SCALE2,
                dot_nt(qx_ref[0:ROWS, cols], a_ref[0:128, cols]) * SCALE2 + 1.0,
            ],
            axis=1,
        )
        m = jnp.max(s, axis=1, keepdims=True)
        e = jnp.exp2(s - m)
        l_ref[:, cols] = wide(jnp.sum(e, axis=1, keepdims=True))
        m_ref[:, cols] = wide(m)
        v = jnp.concatenate([v_ref[:, cols], a_ref[128:256, cols]], axis=0)
        n_ref[:, cols] = dot(e.astype(BF), v)


def sibling(level, a_ref, u_ref, e_ref, cols):
    if level == 1:
        return a_ref[0:128, cols], a_ref[128:256, cols]
    keys = [ref[at : at + n, cols] for ref in (u_ref, e_ref) for at, n in SPANS[level]]
    vals = [ref[at + n : at + 2 * n, cols] for ref in (u_ref, e_ref) for at, n in SPANS[level]]
    return jnp.concatenate(keys, axis=0), jnp.concatenate(vals, axis=0)


def forward_kernel(qx_ref, u_ref, e_ref, n_ref, m_ref, l_ref, att_ref, lse_ref):
    for h in range(qx_ref.shape[1] // HDIM):
        cols = slice(h * HDIM, (h + 1) * HDIM)
        scores, vals = [], []
        for level in range(2, 5):
            k, v = sibling(level, None, u_ref, e_ref, cols)
            q = qx_ref[(level - 1) * ROWS : level * ROWS, cols]
            scores.append(dot_nt(q, k) * SCALE2 + float(level))
            vals.append(v)
        s = jnp.concatenate(scores, axis=1)
        m0 = m_ref[:, cols]
        top = jnp.maximum(m0, wide(jnp.max(s, axis=1, keepdims=True)))
        e = jnp.exp2(s - jnp.concatenate([top] * 3, axis=1))
        own = jnp.exp2(m0 - top)
        total = own * l_ref[:, cols] + wide(jnp.sum(e, axis=1, keepdims=True))
        num = own * n_ref[:, cols] + dot(e.astype(BF), jnp.concatenate(vals, axis=0))
        att_ref[:, cols] = (num / total).astype(BF)
        lse_ref[:, cols] = top + jnp.log2(total)


def row_form(datt_ref, att_ref, lse_ref, cols):
    datt = datt_ref[:, cols].astype(F32)
    delta = jnp.sum(datt * att_ref[:, cols].astype(F32), axis=1, keepdims=True)
    return wide(delta).T[0:1, :], lse_ref[:, cols].T[0:1, :]


def back_kernel(
    qx_ref, a_ref, u_ref, e_ref, datt_ref, att_ref, lse_ref, send_ref, keep_ref, dq_ref, avg_ref
):
    @pl.when(pl.program_id(0) == 0)
    def _():
        for level in range(1, 5):
            avg_ref[(level - 1) * ROWS : level * ROWS, :] = average_matrix(level)

    all_keys, all_ds = [], []
    for h in range(qx_ref.shape[1] // HDIM):
        cols = slice(h * HDIM, (h + 1) * HDIM)
        datt = datt_ref[:, cols]
        delta, lse = row_form(datt_ref, att_ref, lse_ref, cols)
        sides = [sibling(level, a_ref, u_ref, e_ref, cols) for level in range(1, 5)]
        queries = [qx_ref[n * ROWS : (n + 1) * ROWS, cols] for n in range(4)]
        keys = [k for k, _ in sides]
        vals = jnp.concatenate([v for _, v in sides], axis=0)
        scores = [dot_nt(keys[n], queries[n]) * SCALE2 + float(n + 1) for n in range(4)]
        p = jnp.exp2(jnp.concatenate(scores, axis=0) - lse)
        ds = (p * (dot_nt(vals, datt) - delta)).astype(BF)
        gv = dot(p.astype(BF), datt)
        ds = [ds[n * 128 : (n + 1) * 128] for n in range(4)]
        all_keys.append(jnp.concatenate(keys, axis=0).T)
        all_ds.append(ds)
        for level in range(1, 5):
            gk_l = dot(ds[level - 1], queries[level - 1]) * SCALE
            gv_l = gv[(level - 1) * 128 : level * 128]
            if level == 1:
                send_ref[0:128, cols] = gk_l.astype(BF)
                send_ref[128:256, cols] = gv_l.astype(BF)
            else:
                row = 0
                for ref, off in ((keep_ref, 0), (send_ref, 256)):
                    for start, n in SPANS[level]:
                        to = off + start
                        ref[to : to + n, cols] = gk_l[row : row + n].astype(ref.dtype)
                        ref[to + n : to + 2 * n, cols] = gv_l[row : row + n].astype(ref.dtype)
                        row += n
    means = []
    for n in range(4):
        stacked = jnp.concatenate([ds[n] for ds in all_ds], axis=0)
        means.append(dot(stacked, avg_ref[n * ROWS : (n + 1) * ROWS, :]).astype(BF))
    for h in range(qx_ref.shape[1] // HDIM):
        rows = slice(h * 128, (h + 1) * 128)
        gq = dot(all_keys[h], jnp.concatenate([m[rows] for m in means], axis=0))
        dq_ref[:, h * HDIM : (h + 1) * HDIM] = gq.T * SCALE


def local_back_kernel(
    q_ref, k_ref, v_ref, datt_ref, att_ref, lse_ref, gq_ref, dq_ref, gk_ref, gv_ref
):
    for h in range(q_ref.shape[1] // HDIM):
        cols = slice(h * HDIM, (h + 1) * HDIM)
        q, k, v, datt = q_ref[:, cols], k_ref[:, cols], v_ref[:, cols], datt_ref[:, cols]
        delta, lse = row_form(datt_ref, att_ref, lse_ref, cols)
        p = jnp.exp2(dot_nt(k, q) * SCALE2 - lse)
        ds = (p * (dot_nt(v, datt) - delta)).astype(BF)
        gk_ref[:, cols] = dot(ds, q) * SCALE
        gv_ref[:, cols] = dot(p.astype(BF), datt)
        gq = dot(k.T, ds)
        dq_ref[:, cols] = (gq_ref[:, cols] + gq.T * SCALE).astype(BF)


def weight_kernel(own_ref, other_ref, att_ref, attp_ref, *outs):
    x = lax.axis_index("dp") & 3

    def heads(ref, half):
        blocks = []
        for jx in ORDER_X:
            col = pl.multiple_of(((x ^ jx) * 2 + half) * 128, 128)
            blocks.append(ref[:, pl.ds(col, 128)])
        return jnp.concatenate(blocks, axis=1)

    def term(n, half):
        rows = slice(n * 256, (n + 1) * 256)
        return (dot(own_ref[rows, :], mine[half]) + dot(other_ref[rows, :], theirs[half])).astype(BF)

    mine = [heads(att_ref, half) for half in range(2)]
    theirs = [heads(attp_ref, half) for half in range(2)]
    for n in range(4):
        outs[n][...] = term(n, 0)
        part = term(n, 1)
        for m in range(4):
            outs[4 + m][n * 256 : (n + 1) * 256, :] = part[:, m * 128 : (m + 1) * 128]


def sum_first_kernel(*refs):
    ins, (keep_x, send_x, keep_y, send_y) = refs[:8], refs[8:]
    for n, out in enumerate((keep_x, send_x)):
        cols = slice(n * 256, (n + 1) * 256)
        out[...] = sum(r[:, cols].astype(F32) for r in ins[:4]).astype(out.dtype)
    for n, out in enumerate((keep_y, send_y)):
        rows = slice(n * 512, (n + 1) * 512)
        out[...] = sum(r[rows, :].astype(F32) for r in ins[4:]).astype(out.dtype)


def fold(rows, x):
    parts = [x[n * rows : (n + 1) * rows] for n in range(x.shape[0] // rows)]
    return jnp.concatenate(parts, axis=1)


def unfold(cols, x):
    parts = [x[:, n * cols : (n + 1) * cols] for n in range(x.shape[1] // cols)]
    return jnp.concatenate(parts, axis=0)


def sum_second_kernel(
    in_x, got_x, in_y, got_y, keep_ref, rc_ref,
    keep_x, send_x, keep_y, send_y, z_ref, b3_ref, b4_ref,
):
    for n, out in enumerate((keep_x, send_x)):
        cols = slice(n * 128, (n + 1) * 128)
        out[...] = (in_x[:, cols] + got_x[:, cols].astype(F32)).astype(out.dtype)
    keep_y[...] = in_y[0:256, :] + got_y[0:256, :].astype(F32)
    leaves = in_y[256:512, :] + got_y[256:512, :].astype(F32)
    send_y[0:32, :] = fold(32, leaves).astype(BF)

    def both(at, rows):
        return keep_ref[at : at + rows, :] + rc_ref[256 + at : 256 + at + rows, :].astype(F32)

    send_y[32:64, :] = both(192, 32).astype(BF)
    send_y[64:96, :] = both(320, 32).astype(BF)
    z_ref[0:128, :] = both(0, 128).astype(BF)
    z_ref[128:192, :] = both(256, 64).astype(BF)
    b3_ref[...] = both(128, 64)
    b4_ref[0:32, :] = both(224, 32)
    b4_ref[32:64, :] = both(352, 32)


def sum_third_kernel(in_x, got_x, in_y, got_y, b4_ref, keep_ref, send_ref, s4_ref):
    total_x = in_x[...] + got_x[...].astype(F32)
    total_y = in_y[...] + unfold(128, got_y[0:32, :].astype(F32))
    keep_ref[:, 0:128] = total_x[0:128]
    keep_ref[:, 128:256] = total_y[0:128]
    leaves = jnp.concatenate([total_x[128:256], total_y[128:256]], axis=1)
    send_ref[0:32, :] = fold(32, leaves).astype(BF)
    s4_ref[...] = b4_ref[0:32, :] + got_y[32:64, :].astype(F32)
    send_ref[32:64, :] = (b4_ref[32:64, :] + got_y[64:96, :].astype(F32)).astype(BF)


def sum_fourth_kernel(in_ref, got_ref, s4_ref, g_ref, r4_ref):
    g_ref[...] = (in_ref[...] + unfold(256, got_ref[0:32, :].astype(F32))).astype(BF)
    r4_ref[...] = (s4_ref[...] + got_ref[32:64, :].astype(F32)).astype(BF)


def add_kernel(b3_ref, got_ref, out_ref):
    out_ref[...] = (b3_ref[...] + got_ref[128:192, :].astype(F32)).astype(BF)


def place_kernel(a, b, c, d, out_ref):
    x = lax.axis_index("dp") & 3
    for j, ref in enumerate((a, b, c, d)):
        col = pl.multiple_of((x ^ j) * 256, 256)
        out_ref[:, pl.ds(col, 256)] = ref[...].astype(F32)


def finish_kernel(gk_ref, gv_ref, r1, r2, r3, r4, dk_ref, dv_ref, bufs):
    for h in range(gk_ref.shape[1] // HDIM):
        cols = slice(h * HDIM, (h + 1) * HDIM)
        for which, (g0_ref, out_ref) in enumerate(((gk_ref, dk_ref), (gv_ref, dv_ref))):
            g = None
            for ref, rows in ((r4, 16), (r3, 32), (r2, 64), (r1, 128)):
                own = ref[which * rows : (which + 1) * rows, cols].astype(F32)
                g = own if g is None else own + rep2(bufs.at[2 * h + which], 0.5 * g)
            g = g0_ref[:, cols] + rep2(bufs.at[2 * h + which], 0.5 * g)
            out_ref[:, cols] = g.astype(BF)


def shape(rows, cols, dtype=BF):
    return jax.ShapeDtypeStruct((rows, cols), dtype)


def by_heads(rows, step):
    return pl.BlockSpec((rows, step), lambda i: (0, i))


def whole(rows, cols):
    return pl.BlockSpec((rows, cols), lambda i: (0, 0))


def call(kernel, out, flops=1, moved=1, **kw):
    cost = pl.CostEstimate(flops=int(flops), bytes_accessed=int(moved), transcendentals=0)
    return pl.pallas_call(kernel, out_shape=out, compiler_params=VMEM, cost_estimate=cost, **kw)


def per_device(queries, keys, values, d_out, w_out):
    q, k, v, dout = queries[0], keys[0], values[0], d_out[0]
    step = 2 * HDIM
    grid = (WIDTH // step,)
    hs = functools.partial(by_heads, step=step)

    l1, l2, l3, l4 = call(
        coarsen_kernel,
        [shape(2 * rows, WIDTH) for rows in LEVEL_ROWS],
    )(k, v)
    b4 = swap(l4, "seq", Y3)
    c4 = swap(l4, "seq", Y2)
    b3 = swap(l3, "seq", Y1)
    b2 = swap(l2, "seq", ZLO)
    a1 = swap(l1, "seq", CORE)
    t = jnp.concatenate([b3, c4, b4])
    datt = call(
        project_kernel,
        shape(ROWS, WIDTH),
        grid=grid,
        in_specs=[whole(ROWS, DMODEL), hs(DMODEL)],
        out_specs=hs(ROWS),
    )(dout, w_out)
    t, datt = lax.optimization_barrier((t, datt))
    d = swap(t, "seq", ZLO)
    qx, n0, m0, l0 = call(
        local_kernel,
        flops=8e9,
        moved=20e6,
        out=[shape(4 * ROWS, WIDTH)] + [shape(ROWS, WIDTH, F32)] * 3,
        grid=grid,
        in_specs=[hs(ROWS)] * 3 + [hs(256)],
        out_specs=[hs(4 * ROWS)] + [hs(ROWS)] * 3,
    )(q, k, v, a1)
    b2, n0 = lax.optimization_barrier((b2, n0))
    u = jnp.concatenate([b2, t, d])
    e = swap(u, "seq", CORE)
    own_t, other_t = call(
        arrange_kernel,
        [shape(1024, ROWS)] * 2,
        in_specs=[pl.BlockSpec(memory_space=pltpu.VMEM)],
    )(dout)
    rec_t = swap(other_t, "seq", CORE)
    att, lse = call(
        forward_kernel,
        [shape(ROWS, WIDTH), shape(ROWS, WIDTH, F32)],
        grid=grid,
        in_specs=[hs(4 * ROWS), hs(384), hs(384)] + [hs(ROWS)] * 3,
        out_specs=[hs(ROWS), hs(ROWS)],
    )(qx, u, e, n0, m0, l0)

    attp = swap(att, "seq", CORE)
    o = call(
        weight_kernel,
        [shape(256, 512)] * 4 + [shape(1024, 128)] * 4,
        in_specs=[pl.BlockSpec(memory_space=pltpu.VMEM)] * 4,
    )(own_t, rec_t, att, attp)
    keep_x, send_x, keep_y, send_y = call(
        sum_first_kernel,
        [shape(256, 256, F32), shape(256, 256), shape(512, 128, F32), shape(512, 128)],
    )(
        o[0], swap(o[1], "seq", Y1), swap(o[2], "seq", Y3), swap(o[3], "seq", Y2),
        o[4], swap(o[5], "dp", X3), swap(o[6], "dp", X1), swap(o[7], "dp", X2),
    )
    send, keep, gq = call(
        back_kernel,
        [shape(640, WIDTH), shape(384, WIDTH, F32), shape(ROWS, WIDTH, F32)],
        grid=grid,
        in_specs=[hs(4 * ROWS), hs(256), hs(384), hs(384)] + [hs(ROWS)] * 3,
        out_specs=[hs(640), hs(384), hs(ROWS)],
        scratch_shapes=[pltpu.VMEM((4 * ROWS, ROWS), BF)],
    )(qx, a1, u, e, datt, att, lse)
    send, _ = lax.optimization_barrier((send, send_x))

    rc = swap(send, "seq", CORE)
    dq, gk0, gv0 = call(
        local_back_kernel,
        flops=5e9,
        moved=15e6,
        out=[shape(ROWS, WIDTH)] + [shape(ROWS, WIDTH, F32)] * 2,
        grid=grid,
        in_specs=[hs(ROWS)] * 7,
        out_specs=[hs(ROWS)] * 3,
    )(q, k, v, datt, att, lse, gq)
    keep, gk0 = lax.optimization_barrier((keep, gk0))
    keep_x, next_x, keep_y, next_y, out_z, b3, b4 = call(
        sum_second_kernel,
        [shape(256, 128, F32), shape(256, 128), shape(256, 128, F32), shape(96, WIDTH)]
        + [shape(192, WIDTH), shape(64, WIDTH, F32), shape(64, WIDTH, F32)],
    )(keep_x, swap(send_x, "dp", X1), keep_y, swap(send_y, "seq", Y3), keep, rc)
    rz = swap(out_z, "seq", ZLO)
    r3 = call(add_kernel, shape(64, WIDTH))(b3, rz)
    kept, sent, s4 = call(
        sum_third_kernel, [shape(128, 256, F32), shape(64, WIDTH), shape(32, WIDTH, F32)]
    )(keep_x, swap(next_x, "dp", X3), keep_y, swap(next_y, "seq", Y1), b4)
    g, r4 = call(sum_fourth_kernel, [shape(128, 256), shape(32, WIDTH)])(
        kept, swap(sent, "seq", ZLO), s4
    )
    g, r3 = lax.optimization_barrier((g, r3))
    r3, r4 = swap(r3, "seq", Y1), swap(r4, "seq", Y3)
    g = g.astype(F32) + swap(g, "dp", ZH1).astype(F32)
    g = g.astype(BF)
    g = (g.astype(F32) + swap(g, "dp", ZH3).astype(F32)).astype(BF)
    dk, dv = call(
        finish_kernel,
        flops=3e9,
        moved=8e6,
        out=[shape(ROWS, WIDTH)] * 2,
        grid=grid,
        in_specs=[hs(ROWS)] * 2 + [hs(256), hs(128), hs(64), hs(32)],
        out_specs=[hs(ROWS)] * 2,
        scratch_shapes=[pltpu.VMEM((4, ROWS, HDIM), F32)],
    )(gk0, gv0, rc, rz, r3, r4)
    g2, dk = lax.optimization_barrier((swap(g, "dp", X2), dk))
    dw = call(
        place_kernel,
        shape(128, WIDTH, F32),
        in_specs=[pl.BlockSpec(memory_space=pltpu.VMEM)] * 4,
    )(g, swap(g, "dp", X1), g2, swap(g, "dp", X3))
    return dq[None], dk[None], dv[None], dw


def solution(mesh):
    rows = P("dp", "seq", None)
    return jax.shard_map(
        per_device,
        mesh=mesh,
        in_specs=(rows, rows, rows, rows, P()),
        out_specs=(rows, rows, rows, P("seq", None)),
        check_vma=False,
    )
```

```python
import functools
import math

import jax
import jax.numpy as jnp
from jax import lax
from jax.experimental import pallas as pl
from jax.experimental.pallas import tpu as pltpu
from jax.sharding import PartitionSpec as P

HEADS = 8
HDIM = 128
ROWS = 256
WIDTH = 1024
DMODEL = 2048
SCALE = HDIM**-0.5
SCALE2 = SCALE * math.log2(math.e)
LEVEL_ROWS = (128, 64, 32, 16)
SPANS = {2: ((0, 64),), 3: ((128, 32), (256, 32)), 4: ((192, 16), (224, 16), (320, 16), (352, 16))}
BF = jnp.bfloat16
F32 = jnp.float32

CORE, ZLO, Y1, Y2, Y3 = 1, 2, 4, 8, 12
X1, X2, X3, ZH1, ZH3 = 1, 2, 3, 4, 12
ORDER_X = (0, 3, 1, 2)
ORDER_Y = (0, 1, 3, 2)


def swap(value, axis, mask):
    pairs = [(source, source ^ mask) for source in range(16)]
    return lax.ppermute(value, axis, pairs)


def dot(a, b):
    return jnp.dot(a, b, preferred_element_type=F32)


def dot_nt(a, b):
    return lax.dot_general(a, b, (((1,), (1,)), ((), ())), preferred_element_type=F32)


def dot_tn(a, b):
    return lax.dot_general(a, b, (((0,), (0,)), ((), ())), preferred_element_type=F32)


def pool_matrix(rows):
    r = lax.broadcasted_iota(jnp.int32, (rows, 2 * rows), 0)
    c = lax.broadcasted_iota(jnp.int32, (rows, 2 * rows), 1)
    return jnp.where((c == 2 * r) | (c == 2 * r + 1), 0.5, 0.0).astype(BF)


def coarse_levels(x):
    levels = []
    for rows in LEVEL_ROWS:
        x = dot(pool_matrix(rows), x).astype(BF)
        levels.append(x)
    return levels


def spread_matrix(rows):
    t = lax.broadcasted_iota(jnp.int32, (ROWS, rows), 0)
    r = lax.broadcasted_iota(jnp.int32, (ROWS, rows), 1)
    return jnp.where(t // (ROWS // rows) == r, 1.0, 0.0).astype(BF)


def average_matrix(level):
    a = lax.broadcasted_iota(jnp.int32, (ROWS, ROWS), 0)
    b = lax.broadcasted_iota(jnp.int32, (ROWS, ROWS), 1)
    return jnp.where(a // 2**level == b // 2**level, 2.0**-level, 0.0).astype(BF)


def rep2(buf, x):
    rows, cols = x.shape
    buf[pl.ds(0, rows, stride=2), 0:cols] = x
    buf[pl.ds(1, rows, stride=2), 0:cols] = x
    return buf[0 : 2 * rows, 0:cols]


def wide(column):
    return jnp.broadcast_to(column, (column.shape[0], HDIM))


def coarsen_kernel(k_ref, v_ref, o1, o2, o3, o4):
    ks = coarse_levels(k_ref[...])
    vs = coarse_levels(v_ref[...])
    for out, rows, k, v in zip((o1, o2, o3, o4), LEVEL_ROWS, ks, vs):
        out[0:rows, :] = k
        out[rows : 2 * rows, :] = v


def arrange_kernel(dout_ref, own_ref, other_ref):
    seq = lax.axis_index("seq")
    y, zl, c = seq >> 2, (seq >> 1) & 1, seq & 1
    for n in range(8):
        jy, iz = ORDER_Y[n // 2], n % 2
        base = (y ^ jy) * 4 + (zl ^ iz) * 2
        for ref, core in ((own_ref, c), (other_ref, 1 - c)):
            at = pl.multiple_of((base + core) * 128, 128)
            block = dout_ref[:, pl.ds(at, 128)]
            ref[n * 128 : (n + 1) * 128, :] = block.T


def project_kernel(dout_ref, w_ref, datt_ref):
    datt_ref[...] = dot(dout_ref[...], w_ref[...]).astype(BF)


def local_kernel(q_ref, k_ref, v_ref, a_ref, qx_ref, n_ref, m_ref, l_ref):
    for n, x in enumerate(coarse_levels(q_ref[...])):
        qx_ref[n * ROWS : (n + 1) * ROWS, :] = dot(spread_matrix(x.shape[0]), x).astype(BF)
    for h in range(q_ref.shape[1] // HDIM):
        cols = slice(h * HDIM, (h + 1) * HDIM)
        s = jnp.concatenate(
            [
                dot_nt(q_ref[:, cols], k_ref[:, cols]) * SCALE2,
                dot_nt(qx_ref[0:ROWS, cols], a_ref[0:128, cols]) * SCALE2 + 1.0,
            ],
            axis=1,
        )
        m = jnp.max(s, axis=1, keepdims=True)
        e = jnp.exp2(s - m)
        l_ref[:, cols] = wide(jnp.sum(e, axis=1, keepdims=True))
        m_ref[:, cols] = wide(m)
        v = jnp.concatenate([v_ref[:, cols], a_ref[128:256, cols]], axis=0)
        n_ref[:, cols] = dot(e.astype(BF), v)


def sibling(level, a_ref, u_ref, e_ref, cols):
    if level == 1:
        return a_ref[0:128, cols], a_ref[128:256, cols]
    keys = [ref[at : at + n, cols] for ref in (u_ref, e_ref) for at, n in SPANS[level]]
    vals = [ref[at + n : at + 2 * n, cols] for ref in (u_ref, e_ref) for at, n in SPANS[level]]
    return jnp.concatenate(keys, axis=0), jnp.concatenate(vals, axis=0)


def forward_kernel(qx_ref, u_ref, e_ref, n_ref, m_ref, l_ref, att_ref, lse_ref):
    for h in range(qx_ref.shape[1] // HDIM):
        cols = slice(h * HDIM, (h + 1) * HDIM)
        scores, vals = [], []
        for level in range(2, 5):
            k, v = sibling(level, None, u_ref, e_ref, cols)
            q = qx_ref[(level - 1) * ROWS : level * ROWS, cols]
            scores.append(dot_nt(q, k) * SCALE2 + float(level))
            vals.append(v)
        s = jnp.concatenate(scores, axis=1)
        m0 = m_ref[:, cols]
        top = jnp.maximum(m0, wide(jnp.max(s, axis=1, keepdims=True)))
        e = jnp.exp2(s - jnp.concatenate([top] * 3, axis=1))
        own = jnp.exp2(m0 - top)
        total = own * l_ref[:, cols] + wide(jnp.sum(e, axis=1, keepdims=True))
        num = own * n_ref[:, cols] + dot(e.astype(BF), jnp.concatenate(vals, axis=0))
        att_ref[:, cols] = (num / total).astype(BF)
        lse_ref[:, cols] = top + jnp.log2(total)


def row_form(datt_ref, att_ref, lse_ref, cols):
    datt = datt_ref[:, cols].astype(F32)
    delta = jnp.sum(datt * att_ref[:, cols].astype(F32), axis=1, keepdims=True)
    return wide(delta).T[0:1, :], lse_ref[:, cols].T[0:1, :]


def back_kernel(
    qx_ref, a_ref, u_ref, e_ref, datt_ref, att_ref, lse_ref, send_ref, keep_ref, dq_ref, avg_ref
):
    @pl.when(pl.program_id(0) == 0)
    def _():
        for level in range(1, 5):
            avg_ref[(level - 1) * ROWS : level * ROWS, :] = average_matrix(level)

    all_keys, all_ds = [], []
    for h in range(qx_ref.shape[1] // HDIM):
        cols = slice(h * HDIM, (h + 1) * HDIM)
        datt = datt_ref[:, cols]
        delta, lse = row_form(datt_ref, att_ref, lse_ref, cols)
        sides = [sibling(level, a_ref, u_ref, e_ref, cols) for level in range(1, 5)]
        queries = [qx_ref[n * ROWS : (n + 1) * ROWS, cols] for n in range(4)]
        keys = [k for k, _ in sides]
        vals = jnp.concatenate([v for _, v in sides], axis=0)
        scores = [dot_nt(keys[n], queries[n]) * SCALE2 + float(n + 1) for n in range(4)]
        p = jnp.exp2(jnp.concatenate(scores, axis=0) - lse)
        ds = (p * (dot_nt(vals, datt) - delta)).astype(BF)
        gv = dot(p.astype(BF), datt)
        ds = [ds[n * 128 : (n + 1) * 128] for n in range(4)]
        all_keys.append(jnp.concatenate(keys, axis=0).T)
        all_ds.append(ds)
        for level in range(1, 5):
            gk_l = dot(ds[level - 1], queries[level - 1]) * SCALE
            gv_l = gv[(level - 1) * 128 : level * 128]
            if level == 1:
                send_ref[0:128, cols] = gk_l.astype(BF)
                send_ref[128:256, cols] = gv_l.astype(BF)
            else:
                row = 0
                for ref, off in ((keep_ref, 0), (send_ref, 256)):
                    for start, n in SPANS[level]:
                        to = off + start
                        ref[to : to + n, cols] = gk_l[row : row + n].astype(ref.dtype)
                        ref[to + n : to + 2 * n, cols] = gv_l[row : row + n].astype(ref.dtype)
                        row += n
    means = []
    for n in range(4):
        stacked = jnp.concatenate([ds[n] for ds in all_ds], axis=0)
        means.append(dot(stacked, avg_ref[n * ROWS : (n + 1) * ROWS, :]).astype(BF))
    for h in range(qx_ref.shape[1] // HDIM):
        rows = slice(h * 128, (h + 1) * 128)
        gq = dot(all_keys[h], jnp.concatenate([m[rows] for m in means], axis=0))
        dq_ref[:, h * HDIM : (h + 1) * HDIM] = gq.T * SCALE


def local_back_kernel(
    q_ref, k_ref, v_ref, datt_ref, att_ref, lse_ref, gq_ref, dq_ref, gk_ref, gv_ref
):
    for h in range(q_ref.shape[1] // HDIM):
        cols = slice(h * HDIM, (h + 1) * HDIM)
        q, k, v, datt = q_ref[:, cols], k_ref[:, cols], v_ref[:, cols], datt_ref[:, cols]
        delta, lse = row_form(datt_ref, att_ref, lse_ref, cols)
        p = jnp.exp2(dot_nt(k, q) * SCALE2 - lse)
        ds = (p * (dot_nt(v, datt) - delta)).astype(BF)
        gk_ref[:, cols] = dot(ds, q) * SCALE
        gv_ref[:, cols] = dot(p.astype(BF), datt)
        gq = dot(k.T, ds)
        dq_ref[:, cols] = (gq_ref[:, cols] + gq.T * SCALE).astype(BF)


def weight_kernel(own_ref, other_ref, att_ref, attp_ref, *outs):
    x = lax.axis_index("dp") & 3

    def heads(ref, half):
        blocks = []
        for jx in ORDER_X:
            col = pl.multiple_of(((x ^ jx) * 2 + half) * 128, 128)
            blocks.append(ref[:, pl.ds(col, 128)])
        return jnp.concatenate(blocks, axis=1)

    def term(n, half):
        rows = slice(n * 256, (n + 1) * 256)
        return (dot(own_ref[rows, :], mine[half]) + dot(other_ref[rows, :], theirs[half])).astype(BF)

    mine = [heads(att_ref, half) for half in range(2)]
    theirs = [heads(attp_ref, half) for half in range(2)]
    for n in range(4):
        outs[n][...] = term(n, 0)
        part = term(n, 1)
        for m in range(4):
            outs[4 + m][n * 256 : (n + 1) * 256, :] = part[:, m * 128 : (m + 1) * 128]


def sum_first_kernel(*refs):
    ins, (keep_x, send_x, keep_y, send_y) = refs[:8], refs[8:]
    for n, out in enumerate((keep_x, send_x)):
        cols = slice(n * 256, (n + 1) * 256)
        out[...] = sum(r[:, cols].astype(F32) for r in ins[:4]).astype(out.dtype)
    for n, out in enumerate((keep_y, send_y)):
        rows = slice(n * 512, (n + 1) * 512)
        out[...] = sum(r[rows, :].astype(F32) for r in ins[4:]).astype(out.dtype)


def fold(rows, x):
    parts = [x[n * rows : (n + 1) * rows] for n in range(x.shape[0] // rows)]
    return jnp.concatenate(parts, axis=1)


def unfold(cols, x):
    parts = [x[:, n * cols : (n + 1) * cols] for n in range(x.shape[1] // cols)]
    return jnp.concatenate(parts, axis=0)


def sum_second_kernel(
    in_x, got_x, in_y, got_y, keep_ref, rc_ref,
    keep_x, send_x, keep_y, send_y, z_ref, b3_ref, b4_ref,
):
    for n, out in enumerate((keep_x, send_x)):
        cols = slice(n * 128, (n + 1) * 128)
        out[...] = (in_x[:, cols] + got_x[:, cols].astype(F32)).astype(out.dtype)
    keep_y[...] = in_y[0:256, :] + got_y[0:256, :].astype(F32)
    leaves = in_y[256:512, :] + got_y[256:512, :].astype(F32)
    send_y[0:32, :] = fold(32, leaves).astype(BF)

    def both(at, rows):
        return keep_ref[at : at + rows, :] + rc_ref[256 + at : 256 + at + rows, :].astype(F32)

    send_y[32:64, :] = both(192, 32).astype(BF)
    send_y[64:96, :] = both(320, 32).astype(BF)
    z_ref[0:128, :] = both(0, 128).astype(BF)
    z_ref[128:192, :] = both(256, 64).astype(BF)
    b3_ref[...] = both(128, 64)
    b4_ref[0:32, :] = both(224, 32)
    b4_ref[32:64, :] = both(352, 32)


def sum_third_kernel(in_x, got_x, in_y, got_y, b4_ref, keep_ref, send_ref, s4_ref):
    total_x = in_x[...] + got_x[...].astype(F32)
    total_y = in_y[...] + unfold(128, got_y[0:32, :].astype(F32))
    keep_ref[:, 0:128] = total_x[0:128]
    keep_ref[:, 128:256] = total_y[0:128]
    leaves = jnp.concatenate([total_x[128:256], total_y[128:256]], axis=1)
    send_ref[0:32, :] = fold(32, leaves).astype(BF)
    s4_ref[...] = b4_ref[0:32, :] + got_y[32:64, :].astype(F32)
    send_ref[32:64, :] = (b4_ref[32:64, :] + got_y[64:96, :].astype(F32)).astype(BF)


def sum_fourth_kernel(in_ref, got_ref, s4_ref, g_ref, r4_ref):
    g_ref[...] = (in_ref[...] + unfold(256, got_ref[0:32, :].astype(F32))).astype(BF)
    r4_ref[...] = (s4_ref[...] + got_ref[32:64, :].astype(F32)).astype(BF)


def add_kernel(b3_ref, got_ref, out_ref):
    out_ref[...] = (b3_ref[...] + got_ref[128:192, :].astype(F32)).astype(BF)


def place_kernel(a, b, c, d, out_ref):
    x = lax.axis_index("dp") & 3
    for j, ref in enumerate((a, b, c, d)):
        col = pl.multiple_of((x ^ j) * 256, 256)
        out_ref[:, pl.ds(col, 256)] = ref[...].astype(F32)


def finish_kernel(gk_ref, gv_ref, r1, r2, r3, r4, dk_ref, dv_ref, bufs):
    for h in range(gk_ref.shape[1] // HDIM):
        cols = slice(h * HDIM, (h + 1) * HDIM)
        for which, (g0_ref, out_ref) in enumerate(((gk_ref, dk_ref), (gv_ref, dv_ref))):
            g = None
            for ref, rows in ((r4, 16), (r3, 32), (r2, 64), (r1, 128)):
                own = ref[which * rows : (which + 1) * rows, cols].astype(F32)
                g = own if g is None else own + rep2(bufs.at[2 * h + which], 0.5 * g)
            g = g0_ref[:, cols] + rep2(bufs.at[2 * h + which], 0.5 * g)
            out_ref[:, cols] = g.astype(BF)


def shape(rows, cols, dtype=BF):
    return jax.ShapeDtypeStruct((rows, cols), dtype)


def by_heads(rows, step):
    return pl.BlockSpec((rows, step), lambda i: (0, i))


def whole(rows, cols):
    return pl.BlockSpec((rows, cols), lambda i: (0, 0))


def call(kernel, out, flops=1, moved=1, vmem=16, **kw):
    cost = pl.CostEstimate(flops=int(flops), bytes_accessed=int(moved), transcendentals=0)
    params = pltpu.CompilerParams(vmem_limit_bytes=vmem * 1024 * 1024)
    return pl.pallas_call(kernel, out_shape=out, compiler_params=params, cost_estimate=cost, **kw)


def per_device(queries, keys, values, d_out, w_out):
    q, k, v, dout = queries[0], keys[0], values[0], d_out[0]
    step = 2 * HDIM
    grid = (WIDTH // step,)
    hs = functools.partial(by_heads, step=step)

    l1, l2, l3, l4 = call(
        coarsen_kernel,
        [shape(2 * rows, WIDTH) for rows in LEVEL_ROWS],
    )(k, v)
    b4 = swap(l4, "seq", Y3)
    c4 = swap(l4, "seq", Y2)
    b3 = swap(l3, "seq", Y1)
    b2 = swap(l2, "seq", ZLO)
    a1 = swap(l1, "seq", CORE)
    t = jnp.concatenate([b3, c4, b4])
    datt = call(
        project_kernel,
        shape(ROWS, WIDTH),
        grid=grid,
        in_specs=[whole(ROWS, DMODEL), hs(DMODEL)],
        out_specs=hs(ROWS),
    )(dout, w_out)
    t, datt = lax.optimization_barrier((t, datt))
    d = swap(t, "seq", ZLO)
    qx, n0, m0, l0 = call(
        local_kernel,
        flops=8e9,
        moved=20e6,
        out=[shape(4 * ROWS, WIDTH)] + [shape(ROWS, WIDTH, F32)] * 3,
        grid=grid,
        in_specs=[hs(ROWS)] * 3 + [hs(256)],
        out_specs=[hs(4 * ROWS)] + [hs(ROWS)] * 3,
    )(q, k, v, a1)
    b2, n0 = lax.optimization_barrier((b2, n0))
    u = jnp.concatenate([b2, t, d])
    e = swap(u, "seq", CORE)
    own_t, other_t = call(
        arrange_kernel,
        [shape(1024, ROWS)] * 2,
        in_specs=[pl.BlockSpec(memory_space=pltpu.VMEM)],
    )(dout)
    rec_t = swap(other_t, "seq", CORE)
    att, lse = call(
        forward_kernel,
        [shape(ROWS, WIDTH), shape(ROWS, WIDTH, F32)],
        grid=(2,),
        in_specs=[by_heads(n, 512) for n in (4 * ROWS, 384, 384, ROWS, ROWS, ROWS)],
        out_specs=[by_heads(ROWS, 512)] * 2,
    )(qx, u, e, n0, m0, l0)

    attp = swap(att, "seq", CORE)
    o = call(
        weight_kernel,
        [shape(256, 512)] * 4 + [shape(1024, 128)] * 4,
        in_specs=[pl.BlockSpec(memory_space=pltpu.VMEM)] * 4,
    )(own_t, rec_t, att, attp)
    keep_x, send_x, keep_y, send_y = call(
        sum_first_kernel,
        [shape(256, 256, F32), shape(256, 256), shape(512, 128, F32), shape(512, 128)],
    )(
        o[0], swap(o[1], "seq", Y1), swap(o[2], "seq", Y3), swap(o[3], "seq", Y2),
        o[4], swap(o[5], "dp", X3), swap(o[6], "dp", X1), swap(o[7], "dp", X2),
    )
    send, keep, gq = call(
        back_kernel,
        [shape(640, WIDTH), shape(384, WIDTH, F32), shape(ROWS, WIDTH, F32)],
        grid=grid,
        in_specs=[hs(4 * ROWS), hs(256), hs(384), hs(384)] + [hs(ROWS)] * 3,
        out_specs=[hs(640), hs(384), hs(ROWS)],
        scratch_shapes=[pltpu.VMEM((4 * ROWS, ROWS), BF)],
    )(qx, a1, u, e, datt, att, lse)
    send, _ = lax.optimization_barrier((send, send_x))

    rc = swap(send, "seq", CORE)
    dq, gk0, gv0 = call(
        local_back_kernel,
        flops=5e9,
        moved=15e6,
        out=[shape(ROWS, WIDTH)] + [shape(ROWS, WIDTH, F32)] * 2,
        grid=(2,),
        in_specs=[by_heads(ROWS, 512)] * 7,
        out_specs=[by_heads(ROWS, 512)] * 3,
    )(q, k, v, datt, att, lse, gq)
    keep, gk0 = lax.optimization_barrier((keep, gk0))
    keep_x, next_x, keep_y, next_y, out_z, b3, b4 = call(
        sum_second_kernel,
        [shape(256, 128, F32), shape(256, 128), shape(256, 128, F32), shape(96, WIDTH)]
        + [shape(192, WIDTH), shape(64, WIDTH, F32), shape(64, WIDTH, F32)],
    )(keep_x, swap(send_x, "dp", X1), keep_y, swap(send_y, "seq", Y3), keep, rc)
    rz = swap(out_z, "seq", ZLO)
    r3 = call(add_kernel, shape(64, WIDTH))(b3, rz)
    kept, sent, s4 = call(
        sum_third_kernel, [shape(128, 256, F32), shape(64, WIDTH), shape(32, WIDTH, F32)]
    )(keep_x, swap(next_x, "dp", X3), keep_y, swap(next_y, "seq", Y1), b4)
    g, r4 = call(sum_fourth_kernel, [shape(128, 256), shape(32, WIDTH)])(
        kept, swap(sent, "seq", ZLO), s4
    )
    g, r3 = lax.optimization_barrier((g, r3))
    r3, r4 = swap(r3, "seq", Y1), swap(r4, "seq", Y3)
    g = g.astype(F32) + swap(g, "dp", ZH1).astype(F32)
    g = g.astype(BF)
    g = (g.astype(F32) + swap(g, "dp", ZH3).astype(F32)).astype(BF)
    dk, dv = call(
        finish_kernel,
        flops=3e9,
        moved=8e6,
        out=[shape(ROWS, WIDTH)] * 2,
        grid=grid,
        in_specs=[hs(ROWS)] * 2 + [hs(256), hs(128), hs(64), hs(32)],
        out_specs=[hs(ROWS)] * 2,
        scratch_shapes=[pltpu.VMEM((4, ROWS, HDIM), F32)],
    )(gk0, gv0, rc, rz, r3, r4)
    g2, dk = lax.optimization_barrier((swap(g, "dp", X2), dk))
    dw = call(
        place_kernel,
        shape(128, WIDTH, F32),
        in_specs=[pl.BlockSpec(memory_space=pltpu.VMEM)] * 4,
    )(g, swap(g, "dp", X1), g2, swap(g, "dp", X3))
    return dq[None], dk[None], dv[None], dw


def solution(mesh):
    rows = P("dp", "seq", None)
    return jax.shard_map(
        per_device,
        mesh=mesh,
        in_specs=(rows, rows, rows, rows, P()),
        out_specs=(rows, rows, rows, P("seq", None)),
        check_vma=False,
    )
```
